32 devices in a mesh: pipe: 2 (over core), seq: 16 (over z, y, x).
Axes of the slice: x: 2, y: 2, z: 4, core: 2. Of those that a mesh axis runs over, the one named last changes fastest.
Arguments:
- queries: bfloat16 [2, 1024, 4096], P('pipe', 'seq'), may hold values from -6 to 6
- keys: bfloat16 [2, 1024, 4096], P('pipe', 'seq'), may hold values from -6 to 6
- values: bfloat16 [2, 1024, 4096], P('pipe', 'seq'), may hold values from -6 to 6
- out_weight: bfloat16 [2, 4096, 5120], P('pipe', None, 'seq'), may hold values from -0.375 to 0.375
- head_class: int32 [2, 32], P('pipe'), may hold values from 0 to 1
- kv_blocks: int32 [2, 32, 16, 16], P('pipe'), may hold values from 0 to 15, as said below
- kv_count: int32 [2, 32], P('pipe'), may hold values from 1 to 16, as said below
Outputs:
- handed: bfloat16 [2, 1024, 5120], P('pipe', 'seq')
The draws below stay inside these ranges and needn't reach their ends.
Inputs may be any that keep to these rules, and one draw needn't show every extreme that they name: `kv_blocks`: in every row the entries are distinct, and the first is the query block itself. `kv_count`: in every section some head uses all 16 entries.
All inputs are finite; a program needn't handle non-finite values.
Results may differ from the reference program's by a relative error of at most 0.018.
Values may be sent and summed in bfloat16 or wider, within the bound.
A program may use at most 64 MiB of HBM per device.

```python
import jax
import jax.numpy as jnp
from jax import lax

HEAD_SIZE = 128
DM = 5120
FRAMES = 4
BLOCK = 64
LIVE = 16
SEGMENTS = 2
HEADS = 32
TOKENS = 1024
POS = 256
NB = 16


def query_key_pair(key):
    row_width = HEADS * HEAD_SIZE
    shape_all = (SEGMENTS, TOKENS, row_width)
    query_all = jnp.clip(jax.random.normal(jax.random.fold_in(key, 11), shape_all, jnp.float32), -6.0, 6.0)
    key_all = jnp.clip(jax.random.normal(jax.random.fold_in(key, 12), shape_all, jnp.float32), -6.0, 6.0)
    return (query_all.astype(jnp.bfloat16), key_all.astype(jnp.bfloat16))


def draw_queries(key, part):
    return query_key_pair(key)[0]


def draw_keys(key, part):
    return query_key_pair(key)[1]


def draw_kv_blocks(key, part):
    raw_draw = jax.random.randint(key, (SEGMENTS, HEADS, NB, NB), 0, 2 ** 20, dtype=jnp.int32)
    columns = jnp.arange(NB, dtype=jnp.int32)
    logit_scores = raw_draw * NB + columns[None, None, None, :]
    own_block = columns[:, None] == columns[None, :]
    logit_scores = jnp.where(own_block[None, None, :, :], 2 ** 30, logit_scores)
    unused, chosen = lax.top_k(logit_scores, LIVE)
    return chosen.astype(jnp.int32)


def draw_kv_count(key, part):
    raw_draw = jax.random.randint(jax.random.fold_in(key, 1), (SEGMENTS, HEADS), 0, LIVE, dtype=jnp.int32)
    counts = 1 + raw_draw * raw_draw * raw_draw // (LIVE * LIVE)
    heavy_head = jax.random.randint(jax.random.fold_in(key, 2), (SEGMENTS, 1), 0, HEADS, dtype=jnp.int32)
    head_ids = jnp.arange(HEADS, dtype=jnp.int32)[None, :]
    return jnp.where(head_ids == heavy_head, LIVE, counts).astype(jnp.int32)


def with_ends(entries, key, smallest, top_value):
    shape = entries.shape
    place = [jax.random.randint(jax.random.fold_in(key, axis), (), 0, shape[axis]) for axis in range(len(shape))]
    entries = entries.at[tuple(place)].set(smallest)
    longest = shape.index(max(shape))
    place[longest] = (place[longest] + 1) % shape[longest]
    return entries.at[tuple(place)].set(top_value)


def steps_of(stream_key, dims, cuts, low, top_value):
    level = 1.0
    for dim, parts in cuts:
        heights = jax.random.uniform(jax.random.fold_in(jax.random.fold_in(stream_key, 6), dim), (parts,), jnp.float32, low / len(cuts), top_value / len(cuts))
        level = level * jnp.repeat(jnp.exp(heights), dims[dim] // parts).reshape((-1,) + (1,) * (len(dims) - 1 - dim))
    return level


def bell_draw(own_key, dims, deviation, limit, split=(), held_as=jnp.bfloat16):
    level = steps_of(own_key, dims, split, -0.22, 0.18) if split else 1.0
    values = jax.random.normal(own_key, dims, jnp.float32) * deviation * level
    return jnp.minimum(jnp.maximum(values, -limit), limit).astype(held_as)


def setup_inputs(seed: int = 0) -> dict:
    streams_of = jax.random.split(jax.random.key(seed), 8)
    queries = draw_queries(jax.random.fold_in(streams_of[7], 71), 0)
    keys = draw_keys(jax.random.fold_in(streams_of[7], 71), 0)
    values = bell_draw(streams_of[2], (SEGMENTS, TOKENS, HEADS * HEAD_SIZE), 1.0, 6.0, ((0, 2), (1, 16)))
    out_weight = bell_draw(streams_of[3], (SEGMENTS, HEADS * HEAD_SIZE, DM), (HEADS * HEAD_SIZE // 16) ** -0.5, 0.375, ((0, 2), (2, 16)))
    head_class = with_ends(jax.random.randint(streams_of[4], (SEGMENTS, HEADS), 0, 2), jax.random.fold_in(streams_of[4], 1), 0, 1).astype(jnp.int32)
    kv_blocks = draw_kv_blocks(jax.random.fold_in(streams_of[7], 71), 0)
    kv_count = draw_kv_count(jax.random.fold_in(streams_of[7], 71), 0)
    return {"queries": queries, "keys": keys, "values": values, "out_weight": out_weight, "head_class": head_class, "kv_blocks": kv_blocks, "kv_count": kv_count}


def frame_to_pos(tensor):
    return tensor.reshape(FRAMES, POS, -1).transpose(1, 0, 2).reshape(TOKENS, -1)


def pos_to_frame(tensor):
    return tensor.reshape(POS, FRAMES, -1).transpose(1, 0, 2).reshape(TOKENS, -1)


def one_head(inputs):
    query_rows, key_rows, value_rows, head_kind, blocks, live_count = inputs
    temporal = head_kind == 1
    query_rows = jnp.where(temporal, frame_to_pos(query_rows), query_rows)
    key_rows = jnp.where(temporal, frame_to_pos(key_rows), key_rows)
    value_rows = jnp.where(temporal, frame_to_pos(value_rows), value_rows)
    query_tiles = query_rows.reshape(NB, BLOCK, HEAD_SIZE).astype(jnp.float32)
    key_blocks = key_rows.reshape(NB, BLOCK, HEAD_SIZE)
    value_blocks = value_rows.reshape(NB, BLOCK, HEAD_SIZE)
    selected_keys = key_blocks[blocks].reshape(NB, LIVE * BLOCK, HEAD_SIZE).astype(jnp.float32)
    selected_values = value_blocks[blocks].reshape(NB, LIVE * BLOCK, HEAD_SIZE).astype(jnp.float32)
    logit_scores = jnp.einsum("ure,ute->urt", query_tiles, selected_keys) * (HEAD_SIZE ** -0.5)
    live_mask = jnp.repeat(jnp.arange(LIVE) < live_count, BLOCK)[None, None, :]
    logit_scores = jnp.where(live_mask, logit_scores, -jnp.inf)
    row_max = jnp.max(logit_scores, axis=-1, keepdims=True)
    probs = jnp.where(live_mask, jnp.exp(logit_scores - row_max), 0.0)
    softmax_denominator = jnp.sum(probs, axis=-1, keepdims=True)
    block_probabilities = probs.astype(jnp.bfloat16)
    attended_values = jnp.einsum("yhn,yng->yhg", block_probabilities.astype(jnp.float32), selected_values) / softmax_denominator
    attended_values = attended_values.reshape(TOKENS, HEAD_SIZE)
    attended_values = jnp.where(temporal, pos_to_frame(attended_values), attended_values)
    return attended_values.astype(jnp.bfloat16)


def one_segment(inputs):
    query_rows, key_rows, value_rows, weight, classes, blocks, counts = inputs
    def split_heads(tensor):
        return tensor.reshape(TOKENS, HEADS, HEAD_SIZE).transpose(1, 0, 2)
    result = lax.map(one_head, (split_heads(query_rows), split_heads(key_rows), split_heads(value_rows), classes, blocks, counts))
    attended_values = result.transpose(1, 0, 2).reshape(TOKENS, HEADS * HEAD_SIZE)
    return jnp.dot(attended_values, weight, preferred_element_type=jnp.float32).astype(jnp.bfloat16)


def reference(queries, keys, values, out_weight, head_class, kv_blocks, kv_count):
    projected = lax.map(one_segment, (queries, keys, values, out_weight, head_class, kv_blocks, kv_count))
    return jnp.roll(projected, 1, axis=0)
```

```python
import functools

import jax
import jax.numpy as jnp
from jax import lax
from jax.experimental import pallas as pl
from jax.experimental.pallas import tpu as pltpu
from jax.sharding import PartitionSpec as P

FRAMES = 4
BLOCK = 64
MASKED = 131072.0
LOG2E = 1.4426950408889634
MESH = pl.DeviceIdType.MESH


def kernel(
    members, per_dev, stages,
    classes, counts, lists, queries, keys, values, weight,
    out,
    qbuf, kbuf, vbuf, ebuf, bbuf, abuf, wown, wpart, cown, cpart, csend, crecv, osend, obuf,
    qkv_send, qkv_recv, qkv_local, w_sems, w_local, a_send, f_send, a_recv, c_send, c_recv,
    o_send, o_recv,
):
    stage = lax.axis_index("pipe")
    me = lax.axis_index("seq")
    half = lax.rem(me, 2)
    col = me // 2
    side = lax.rem(col, 2)
    level = col // 2
    levels = members // 4
    partner = me + 1 - 2 * half
    across_col = col + 1 - 2 * side
    across = 2 * across_col + half
    following = lax.rem(stage + 1, stages)
    preceding = lax.rem(stage + stages - 1, stages)
    rows, width = queries.shape[0], kbuf.shape[-1]
    tokens = rows * members
    tensors = ((queries, qbuf), (keys, kbuf), (values, vbuf))

    def level_col(r):
        return lax.rem(level + r, levels) * 2

    barrier = pltpu.get_barrier_semaphore()

    def greet(r, carry):
        pl.semaphore_signal(
            barrier, inc=1, device_id={"seq": lax.rem(me + r, members)}, device_id_type=MESH
        )
        return carry

    def greet_preceding(r, carry):
        pl.semaphore_signal(barrier, inc=1, device_id=(preceding, r), device_id_type=MESH)
        return carry

    lax.fori_loop(1, members, greet, 0)
    lax.fori_loop(0, members, greet_preceding, 0)
    weight_copy = pltpu.make_async_copy(weight.at[:, half], wown, w_local)
    weight_copy.start()

    def head_columns(owner, slot):
        return pl.ds(pl.multiple_of((owner * per_dev + slot) * width, width), width)

    mine = pl.ds(pl.multiple_of(me * rows, rows), rows)
    own_copies = []
    for slot in range(per_dev):
        for which, (source, landing) in enumerate(tensors):
            copy = pltpu.make_async_copy(
                source.at[:, head_columns(me, slot)],
                landing.at[slot, mine],
                qkv_local.at[slot, which],
            )
            copy.start()
            own_copies.append(copy)
    pl.semaphore_wait(barrier, 2 * members - 1)

    for slot in range(per_dev):

        def send(r, carry):
            peer = lax.rem(me + r, members)
            for which, (source, landing) in enumerate(tensors):
                pltpu.make_async_remote_copy(
                    src_ref=source.at[:, head_columns(peer, slot)],
                    dst_ref=landing.at[slot, mine],
                    send_sem=qkv_send.at[slot, which],
                    recv_sem=qkv_recv.at[slot, which],
                    device_id={"seq": peer},
                    device_id_type=MESH,
                ).start()
            return carry

        lax.fori_loop(1, members, send, 0)
    weight_swap = pltpu.make_async_remote_copy(
        src_ref=weight.at[:, 1 - half],
        dst_ref=wpart,
        send_sem=w_sems.at[0],
        recv_sem=w_sems.at[1],
        device_id={"seq": partner},
        device_id_type=MESH,
    )
    weight_swap.start()

    nblock = lists.shape[1]
    token = lax.broadcasted_iota(jnp.int32, (tokens, width), 0)
    lane = lax.broadcasted_iota(jnp.int32, (tokens, width), 1)
    spatial = token // BLOCK
    temporal = lax.rem(token, tokens // FRAMES) // (BLOCK // FRAMES)
    listed_lane = lax.broadcasted_iota(jnp.int32, (nblock, width), 1)
    for slot in range(per_dev):
        head = me * per_dev + slot
        block_of = jnp.where(classes[0, head] == 1, temporal, spatial)
        member = jnp.where(block_of == lane, 1.0, 0.0).astype(jnp.bfloat16)
        ebuf[slot] = member
        entries = lists[head]
        offset = jnp.full((nblock, width), -MASKED, jnp.float32)
        for entry in range(entries.shape[1]):
            level_here = jnp.where(entry < counts[0, head], 0.0, -MASKED)
            offset = jnp.maximum(
                offset, jnp.where(entries[:, entry : entry + 1] == listed_lane, level_here, -MASKED)
            )
        offset = jnp.concatenate(
            [offset, jnp.zeros((width - nblock, width), jnp.float32)], axis=0
        ).astype(jnp.bfloat16)
        bbuf[slot] = lax.dot_general(
            member, offset, (((1,), (1,)), ((), ())), preferred_element_type=jnp.float32
        ).astype(jnp.bfloat16)
    cown[...] = jnp.zeros_like(cown)
    cpart[...] = jnp.zeros_like(cpart)
    for copy in own_copies:
        copy.wait()

    tile = 256
    scale = LOG2E * width ** (-0.5)
    others = pl.ds(0, tokens - rows)

    def shard_copy(source_col, slot, target, send_sem):
        return pltpu.make_async_remote_copy(
            src_ref=abuf.at[source_col, slot],
            dst_ref=abuf.at[source_col, slot],
            send_sem=send_sem,
            recv_sem=a_recv.at[source_col, slot],
            device_id={"seq": target},
            device_id_type=MESH,
        )

    def received(source_col, slot):
        pltpu.make_async_copy(
            abuf.at[source_col, slot], abuf.at[source_col, slot], a_recv.at[source_col, slot]
        ).wait()

    for slot in range(per_dev):
        for which, (source, landing) in enumerate(tensors):
            span = landing.at[slot, others]
            pltpu.make_async_copy(span, span, qkv_recv.at[slot, which]).wait()

        def attend(step, carry):
            here = pl.ds(pl.multiple_of(step * tile, tile), tile)
            wide_query = jnp.concatenate([qbuf[slot, here], ebuf[slot, here]], axis=1)
            wide_key = jnp.concatenate([kbuf[slot], bbuf[slot]], axis=1)
            scores = lax.dot_general(
                wide_query, wide_key, (((1,), (1,)), ((), ())), preferred_element_type=jnp.float32
            )
            top = jnp.max(scores, axis=1, keepdims=True)
            probs = jnp.exp2((scores - top) * scale).astype(jnp.bfloat16)
            wide_value = jnp.concatenate(
                [vbuf[slot], jnp.ones((tokens, width), jnp.bfloat16)], axis=1
            )
            sums = jnp.dot(probs, wide_value, preferred_element_type=jnp.float32)
            abuf[col, slot, here] = (sums[:, :width] / sums[:, width:]).astype(jnp.bfloat16)
            return carry

        lax.fori_loop(0, tokens // tile, attend, 0)
        shard_copy(col, slot, across, a_send.at[slot, 0]).start()

        def spread(r, carry):
            shard_copy(col, slot, 2 * (level_col(r) + side) + half, a_send.at[slot, r]).start()
            return carry

        lax.fori_loop(1, levels, spread, 0)

    weight_copy.wait()
    weight_swap.wait_recv()

    def shares(source_col, here):
        piece = jnp.concatenate([abuf[source_col, s, here] for s in range(per_dev)], axis=1)
        return (
            jnp.dot(piece, wown[source_col], preferred_element_type=jnp.float32),
            jnp.dot(piece, wpart[source_col], preferred_element_type=jnp.float32),
        )

    def accumulate(source_col):
        def part(step, carry):
            here = pl.ds(pl.multiple_of(step * tile, tile), tile)
            to_own, to_part = shares(source_col, here)
            cown[here] += to_own
            cpart[here] += to_part
            return carry

        lax.fori_loop(0, tokens // tile, part, 0)

    accumulate(col)

    def pass_on(r, carry):
        source_col = level_col(r) + side
        for slot in range(per_dev):
            received(source_col, slot)
            shard_copy(source_col, slot, across, f_send.at[slot, r]).start()
        accumulate(source_col)
        return carry

    lax.fori_loop(1, levels, pass_on, 0)

    def take_in(r, carry):
        source_col = level_col(r) + 1 - side
        for slot in range(per_dev):
            received(source_col, slot)
        accumulate(source_col)
        return carry

    lax.fori_loop(0, levels - 1, take_in, 0)
    last_col = level_col(levels - 1) + 1 - side
    for slot in range(per_dev):
        received(last_col, slot)

    chunks = tokens // tile

    def chunk_copy(here, chunk):
        return pltpu.make_async_remote_copy(
            src_ref=csend.at[here],
            dst_ref=crecv.at[here],
            send_sem=c_send.at[chunk],
            recv_sem=c_recv.at[chunk],
            device_id={"seq": partner},
            device_id_type=MESH,
        )

    def chunk_rows(chunk):
        return pl.ds(pl.multiple_of(chunk * tile, tile), tile)

    def finish(step, carry):
        chunk = lax.rem(step + col, chunks)
        here = chunk_rows(chunk)
        to_own, to_part = shares(last_col, here)
        csend[here] = (cpart[here] + to_part).astype(jnp.bfloat16)
        chunk_copy(here, chunk).start()
        cown[here] += to_own
        return carry

    lax.fori_loop(0, chunks, finish, 0)

    def row_copy(owner):
        return pltpu.make_async_remote_copy(
            src_ref=osend.at[pl.ds(pl.multiple_of(owner * rows, rows), rows)],
            dst_ref=obuf.at[me],
            send_sem=o_send.at[owner],
            recv_sem=o_recv.at[me],
            device_id=(following, owner),
            device_id_type=MESH,
        )

    def hand(step, carry):
        chunk = lax.rem(step + col, chunks)
        here = chunk_rows(chunk)
        chunk_copy(here, chunk).wait_recv()
        osend[here] = (cown[here] + crecv[here].astype(jnp.float32)).astype(jnp.bfloat16)
        for owner in range(tile // rows):
            row_copy(chunk * (tile // rows) + owner).start()
        return carry

    lax.fori_loop(0, chunks, hand, 0)

    for slot in range(per_dev):
        for which, (source, landing) in enumerate(tensors):
            span = landing.at[slot, others]
            pltpu.make_async_copy(span, span, qkv_send.at[slot, which]).wait()
        shard_copy(col, slot, across, a_send.at[slot, 0]).wait_send()

        def left(r, carry):
            shard_copy(col, slot, across, a_send.at[slot, r]).wait_send()
            shard_copy(level_col(r) + side, slot, across, f_send.at[slot, r]).wait_send()
            return carry

        lax.fori_loop(1, levels, left, 0)
    weight_swap.wait_send()

    def chunk_left(chunk, carry):
        chunk_copy(chunk_rows(chunk), chunk).wait_send()
        return carry

    lax.fori_loop(0, chunks, chunk_left, 0)

    def arrived(source, carry):
        row_copy(source).wait_send()
        pltpu.make_async_copy(obuf.at[source], obuf.at[source], o_recv.at[source]).wait()
        return carry

    lax.fori_loop(0, members, arrived, 0)
    pair = 2 * obuf.shape[2]
    for i in range(members // 2):
        out[:, i * pair : (i + 1) * pair] = jnp.concatenate([obuf[2 * i], obuf[2 * i + 1]], axis=1)


def shards(stages, queries, keys, values, out_weight, head_class, kv_blocks, kv_count):
    members = lax.axis_size("seq")
    heads = head_class.shape[1]
    per_dev = heads // members
    rows, total = queries.shape[1:]
    width = total // heads
    tokens = rows * members
    out_cols = out_weight.shape[2]
    cols = members // 2
    depth = per_dev * width
    weight = out_weight[0].reshape(cols, 2, depth, out_cols)
    bf16, f32 = jnp.bfloat16, jnp.float32
    dma = pltpu.SemaphoreType.DMA
    vmem = pl.BlockSpec(memory_space=pltpu.VMEM)
    smem = pl.BlockSpec(memory_space=pltpu.SMEM)
    head_buffer = pltpu.VMEM((per_dev, tokens, width), bf16)
    levels = members // 4
    chunks = tokens // 256
    result = pl.pallas_call(
        functools.partial(kernel, members, per_dev, stages),
        out_shape=jax.ShapeDtypeStruct((rows, members * out_cols), bf16),
        in_specs=[smem, smem, vmem, vmem, vmem, vmem, pl.BlockSpec(memory_space=pl.ANY)],
        out_specs=vmem,
        scratch_shapes=[
            head_buffer, head_buffer, head_buffer, head_buffer, head_buffer,
            pltpu.VMEM((cols, per_dev, tokens, width), bf16),
            pltpu.VMEM((cols, depth, out_cols), bf16),
            pltpu.VMEM((cols, depth, out_cols), bf16),
            pltpu.VMEM((tokens, out_cols), f32),
            pltpu.VMEM((tokens, out_cols), f32),
            pltpu.VMEM((tokens, out_cols), bf16),
            pltpu.VMEM((tokens, out_cols), bf16),
            pltpu.VMEM((tokens, out_cols), bf16),
            pltpu.VMEM((members, rows, out_cols), bf16),
            dma((per_dev, 3)), dma((per_dev, 3)), dma((per_dev, 3)),
            dma((2,)), dma,
            dma((per_dev, levels)), dma((per_dev, levels)), dma((cols, per_dev)),
            dma((chunks,)), dma((chunks,)),
            dma((members,)), dma((members,)),
        ],
        compiler_params=pltpu.CompilerParams(
            collective_id=0, has_side_effects=True, vmem_limit_bytes=48 * 1024 * 1024
        ),
        cost_estimate=pl.CostEstimate(
            flops=4 * tokens * tokens * depth + 2 * tokens * total * out_cols,
            bytes_accessed=2 * (3 * rows * total + total * out_cols + rows * members * out_cols),
            transcendentals=per_dev * tokens * tokens,
        ),
    )(head_class, kv_count, kv_blocks[0], queries[0], keys[0], values[0], weight)
    return result[None]


def solution(mesh):
    placed = (
        P("pipe", "seq", None),
        P("pipe", "seq", None),
        P("pipe", "seq", None),
        P("pipe", None, "seq"),
        P("pipe", None),
        P("pipe", None, None, None),
        P("pipe", None),
    )
    return jax.shard_map(
        functools.partial(shards, mesh.shape["pipe"]),
        mesh=mesh, in_specs=placed, out_specs=P("pipe", "seq", None), check_vma=False,
    )
```

```python
import functools

import jax
import jax.numpy as jnp
from jax import lax
from jax.experimental import pallas as pl
from jax.experimental.pallas import tpu as pltpu
from jax.sharding import PartitionSpec as P

FRAMES = 4
BLOCK = 64
MASKED = 131072.0
LOG2E = 1.4426950408889634
TILE = 256
MESH = pl.DeviceIdType.MESH


def kernel(
    members, per_dev, stages,
    classes, counts, lists, queries, keys, values, weight,
    out,
    qbuf, kbuf, vbuf, ebuf, bbuf, abuf, wboth, cown, csend, crecv, osend, obuf,
    qkv_send, qkv_recv, qkv_local, w_sems, w_local, up_send, down_send, side_send, a_recv,
    c_send, c_recv, o_send, o_recv,
):
    stage = lax.axis_index("pipe")
    me = lax.axis_index("seq")
    half = lax.rem(me, 2)
    col = me // 2
    side = lax.rem(col, 2)
    level = col // 2
    levels = members // 4
    cols = members // 2
    partner = me + 1 - 2 * half
    across = me + 2 - 4 * side
    following = lax.rem(stage + 1, stages)
    preceding = lax.rem(stage + stages - 1, stages)
    rows, width = queries.shape[0], kbuf.shape[-1]
    tokens = rows * members
    depth = per_dev * width
    out_cols = weight.shape[0]
    tile = TILE
    chunks = tokens // tile
    group = tile // rows
    tensors = ((queries, qbuf), (keys, kbuf), (values, vbuf))

    def block_at(chunk, place):
        return place * chunks + lax.rem(chunk + place, chunks)

    barrier = pltpu.get_barrier_semaphore()

    def greet(r, carry):
        pl.semaphore_signal(
            barrier, inc=1, device_id={"seq": lax.rem(me + r, members)}, device_id_type=MESH
        )
        return carry

    def greet_preceding(r, carry):
        pl.semaphore_signal(barrier, inc=1, device_id=(preceding, r), device_id_type=MESH)
        return carry

    lax.fori_loop(1, members, greet, 0)
    lax.fori_loop(0, members, greet_preceding, 0)

    def head_columns(owner, slot):
        return pl.ds(pl.multiple_of((owner * per_dev + slot) * width, width), width)

    my_place = me // chunks
    my_chunk = lax.rem(lax.rem(me, chunks) + chunks * group - my_place, chunks)
    mine = pl.ds(pl.multiple_of((my_chunk * group + my_place) * rows, rows), rows)
    own_copies = []
    for slot in range(per_dev):
        for which, (source, landing) in enumerate(tensors):
            copy = pltpu.make_async_copy(
                source.at[:, head_columns(me, slot)],
                landing.at[slot, mine],
                qkv_local.at[slot, which],
            )
            copy.start()
            own_copies.append(copy)
    pl.semaphore_wait(barrier, 2 * members - 1)

    for slot in range(per_dev):

        def send(r, carry):
            peer = lax.rem(me + r, members)
            for which, (source, landing) in enumerate(tensors):
                pltpu.make_async_remote_copy(
                    src_ref=source.at[:, head_columns(peer, slot)],
                    dst_ref=landing.at[slot, mine],
                    send_sem=qkv_send.at[slot, which],
                    recv_sem=qkv_recv.at[slot, which],
                    device_id={"seq": peer},
                    device_id_type=MESH,
                ).start()
            return carry

        lax.fori_loop(1, members, send, 0)

    def weight_columns(column, which_half):
        return pl.ds(pl.multiple_of((2 * column + which_half) * depth, depth), depth)

    def own_weight(column, carry):
        pltpu.make_async_copy(
            weight.at[:, weight_columns(column, half)],
            wboth.at[pl.ds(0, out_cols), pl.ds(pl.multiple_of(column * depth, depth), depth)],
            w_local,
        ).start()
        return carry

    lax.fori_loop(0, cols, own_weight, 0)

    nblock = lists.shape[0]
    place = lax.broadcasted_iota(jnp.int32, (tokens, width), 0)
    lane = lax.broadcasted_iota(jnp.int32, (tokens, width), 1)
    token = block_at(place // tile, lax.rem(place, tile) // rows) * rows + lax.rem(place, rows)
    spatial = token // BLOCK
    temporal = lax.rem(token, tokens // FRAMES) // (BLOCK // FRAMES)
    every = lists[...].astype(jnp.float32)
    head_lane = lax.broadcasted_iota(jnp.int32, every.shape, 2)
    entry = lax.broadcasted_iota(jnp.int32, every.shape[:2] + (width,), 1)
    listed_lane = lax.broadcasted_iota(jnp.int32, entry.shape, 2).astype(jnp.float32)
    for slot in range(per_dev):
        head = me * per_dev + slot
        block_of = jnp.where(classes[0, head] == 1, temporal, spatial)
        member = jnp.where(block_of == lane, 1.0, 0.0).astype(jnp.bfloat16)
        ebuf[slot] = member
        entries = jnp.sum(jnp.where(head_lane == head, every, 0.0), axis=2, keepdims=True)
        usable = jnp.where(entry < counts[0, head], 0.0, -MASKED)
        offset = jnp.max(jnp.where(entries == listed_lane, usable, -MASKED), axis=1)
        offset = jnp.concatenate(
            [offset, jnp.zeros((width - nblock, width), jnp.float32)], axis=0
        ).astype(jnp.bfloat16)
        bbuf[slot] = lax.dot_general(
            member, offset, (((1,), (1,)), ((), ())), preferred_element_type=jnp.float32
        ).astype(jnp.bfloat16)
    for copy in own_copies:
        copy.wait()

    scale = LOG2E * width ** (-0.5)
    others = pl.ds(0, tokens - rows)

    def chunk_rows(chunk):
        return pl.ds(pl.multiple_of(chunk * tile, tile), tile)

    def piece_copy(source_level, slot, chunk, target, sems):
        column = 2 * source_level + side
        piece = abuf.at[column, slot, chunk_rows(chunk)]
        return pltpu.make_async_remote_copy(
            src_ref=piece,
            dst_ref=piece,
            send_sem=sems.at[slot, chunk, source_level],
            recv_sem=a_recv.at[column, slot, chunk],
            device_id={"seq": target},
            device_id_type=MESH,
        )

    def received(column, slot, chunk):
        piece = abuf.at[column, slot, chunk_rows(chunk)]
        pltpu.make_async_copy(piece, piece, a_recv.at[column, slot, chunk]).wait()

    def send_up(source_level, slot, chunk):
        @pl.when(level + 1 < levels)
        def _():
            piece_copy(source_level, slot, chunk, me + 4, up_send).start()

    def send_down(source_level, slot, chunk):
        @pl.when(level >= 1)
        def _():
            piece_copy(source_level, slot, chunk, me - 4, down_send).start()

    def send_side(source_level, slot, chunk):
        piece_copy(source_level, slot, chunk, across, side_send).start()

    def attend(slot):
        for which, (source, landing) in enumerate(tensors):
            span = landing.at[slot, others]
            pltpu.make_async_copy(span, span, qkv_recv.at[slot, which]).wait()

        def step(chunk, carry):
            here = chunk_rows(chunk)
            wide_query = jnp.concatenate([qbuf[slot, here], ebuf[slot, here]], axis=1)
            wide_key = jnp.concatenate([kbuf[slot], bbuf[slot]], axis=1)
            scores = lax.dot_general(
                wide_query, wide_key, (((1,), (1,)), ((), ())), preferred_element_type=jnp.float32
            )
            top = jnp.max(scores, axis=1, keepdims=True)
            probs = jnp.exp2((scores - top) * scale).astype(jnp.bfloat16)
            wide_value = jnp.concatenate(
                [vbuf[slot], jnp.ones((tokens, width), jnp.bfloat16)], axis=1
            )
            sums = jnp.dot(probs, wide_value, preferred_element_type=jnp.float32)
            abuf[col, slot, here] = (sums[:, :width] / sums[:, width:]).astype(jnp.bfloat16)
            send_up(level, slot, chunk)
            send_down(level, slot, chunk)
            send_side(level, slot, chunk)
            return carry

        lax.fori_loop(0, chunks, step, 0)

    def relay(slot, chunk):
        def hop(t, carry):
            below = level - 1 - t
            above = level + 1 + t

            @pl.when(below >= 0)
            def _():
                received(2 * below + side, slot, chunk)
                send_up(below, slot, chunk)
                send_side(below, slot, chunk)

            @pl.when(above < levels)
            def _():
                received(2 * above + side, slot, chunk)
                send_down(above, slot, chunk)
                send_side(above, slot, chunk)

            return carry

        lax.fori_loop(0, levels - 1, hop, 0)

    weight_span = wboth.at[pl.ds(out_cols, out_cols)]
    for slot in range(per_dev):
        attend(slot)
        if slot == 0:

            def swap_weight(column, carry):
                pltpu.make_async_remote_copy(
                    src_ref=weight.at[:, weight_columns(column, 1 - half)],
                    dst_ref=wboth.at[
                        pl.ds(out_cols, out_cols),
                        pl.ds(pl.multiple_of(column * depth, depth), depth),
                    ],
                    send_sem=w_sems.at[0],
                    recv_sem=w_sems.at[1],
                    device_id={"seq": partner},
                    device_id_type=MESH,
                ).start()
                return carry

            lax.fori_loop(0, cols, swap_weight, 0)
        if slot < per_dev - 1:

            def relay_step(chunk, carry):
                relay(slot, chunk)
                return carry

            lax.fori_loop(0, chunks, relay_step, 0)

    weight_own = wboth.at[pl.ds(0, out_cols)]
    pltpu.make_async_copy(weight_own, weight_own, w_local).wait()
    pltpu.make_async_copy(weight_span, weight_span, w_sems.at[1]).wait()

    def chunk_copy(chunk):
        here = chunk_rows(chunk)
        return pltpu.make_async_remote_copy(
            src_ref=csend.at[here],
            dst_ref=crecv.at[here],
            send_sem=c_send.at[chunk],
            recv_sem=c_recv.at[chunk],
            device_id={"seq": partner},
            device_id_type=MESH,
        )

    def row_copy(chunk, q):
        start = pl.multiple_of((chunk * group + q) * rows, rows)
        return pltpu.make_async_remote_copy(
            src_ref=osend.at[pl.ds(start, rows)],
            dst_ref=obuf.at[me],
            send_sem=o_send.at[chunk * group + q],
            recv_sem=o_recv.at[me],
            device_id=(following, block_at(chunk, q)),
            device_id_type=MESH,
        )

    def hand(chunk):
        here = chunk_rows(chunk)
        chunk_copy(chunk).wait_recv()
        osend[here] = (cown[here] + crecv[here].astype(jnp.float32)).astype(jnp.bfloat16)
        for q in range(group):
            row_copy(chunk, q).start()

    def finish(chunk, carry):
        here = chunk_rows(chunk)
        relay(per_dev - 1, chunk)

        def from_side(source_level, inner):
            for slot in range(per_dev):
                received(2 * source_level + 1 - side, slot, chunk)
            return inner

        lax.fori_loop(0, levels, from_side, 0)
        piece = jnp.concatenate(
            [abuf[column, slot, here] for column in range(cols) for slot in range(per_dev)], axis=1
        )
        shares = lax.dot_general(
            piece, wboth[...], (((1,), (1,)), ((), ())), preferred_element_type=jnp.float32
        )
        csend[here] = shares[:, out_cols:].astype(jnp.bfloat16)
        chunk_copy(chunk).start()
        cown[here] = shares[:, :out_cols]

        @pl.when(chunk >= 1)
        def _():
            hand(chunk - 1)

        return carry

    lax.fori_loop(0, chunks, finish, 0)
    hand(chunks - 1)

    for slot in range(per_dev):
        for which, (source, landing) in enumerate(tensors):
            span = landing.at[slot, others]
            pltpu.make_async_copy(span, span, qkv_send.at[slot, which]).wait()
    pltpu.make_async_copy(weight_span, weight_span, w_sems.at[0]).wait()

    def left(chunk, carry):
        for slot in range(per_dev):

            def from_level(source_level, inner):
                @pl.when((level + 1 < levels) & (source_level <= level))
                def _():
                    piece_copy(source_level, slot, chunk, across, up_send).wait_send()

                @pl.when((level >= 1) & (source_level >= level))
                def _():
                    piece_copy(source_level, slot, chunk, across, down_send).wait_send()

                piece_copy(source_level, slot, chunk, across, side_send).wait_send()
                return inner

            lax.fori_loop(0, levels, from_level, 0)
        chunk_copy(chunk).wait_send()
        for q in range(group):
            row_copy(chunk, q).wait_send()
        return carry

    lax.fori_loop(0, chunks, left, 0)

    def arrived(source, carry):
        pltpu.make_async_copy(obuf.at[source], obuf.at[source], o_recv.at[source]).wait()
        return carry

    lax.fori_loop(0, members, arrived, 0)
    pair = 2 * out_cols
    for i in range(members // 2):
        out[:, i * pair : (i + 1) * pair] = jnp.concatenate([obuf[2 * i], obuf[2 * i + 1]], axis=1)


def shards(stages, queries, keys, values, out_weight, head_class, kv_blocks, kv_count):
    members = lax.axis_size("seq")
    heads = head_class.shape[1]
    per_dev = heads // members
    rows, total = queries.shape[1:]
    width = total // heads
    tokens = rows * members
    out_cols = out_weight.shape[2]
    cols = members // 2
    depth = per_dev * width
    weight = out_weight[0].T
    bf16, f32 = jnp.bfloat16, jnp.float32
    dma = pltpu.SemaphoreType.DMA
    vmem = pl.BlockSpec(memory_space=pltpu.VMEM)
    smem = pl.BlockSpec(memory_space=pltpu.SMEM)
    hbm = pl.BlockSpec(memory_space=pl.ANY)
    head_buffer = pltpu.VMEM((per_dev, tokens, width), bf16)
    levels = members // 4
    chunks = tokens // TILE
    result = pl.pallas_call(
        functools.partial(kernel, members, per_dev, stages),
        out_shape=jax.ShapeDtypeStruct((rows, members * out_cols), bf16),
        in_specs=[smem, smem, vmem, hbm, hbm, hbm, hbm],
        out_specs=vmem,
        scratch_shapes=[
            head_buffer, head_buffer, head_buffer, head_buffer, head_buffer,
            pltpu.VMEM((cols, per_dev, tokens, width), bf16),
            pltpu.VMEM((2 * out_cols, cols * depth), bf16),
            pltpu.VMEM((tokens, out_cols), f32),
            pltpu.VMEM((tokens, out_cols), bf16),
            pltpu.VMEM((tokens, out_cols), bf16),
            pltpu.VMEM((tokens, out_cols), bf16),
            pltpu.VMEM((members, rows, out_cols), bf16),
            dma((per_dev, 3)), dma((per_dev, 3)), dma((per_dev, 3)),
            dma((2,)), dma,
            dma((per_dev, chunks, levels)), dma((per_dev, chunks, levels)),
            dma((per_dev, chunks, levels)), dma((cols, per_dev, chunks)),
            dma((chunks,)), dma((chunks,)),
            dma((members,)), dma((members,)),
        ],
        compiler_params=pltpu.CompilerParams(
            collective_id=0, has_side_effects=True, vmem_limit_bytes=60 * 1024 * 1024
        ),
        cost_estimate=pl.CostEstimate(
            flops=4 * tokens * tokens * depth + 2 * tokens * total * out_cols,
            bytes_accessed=2 * (3 * rows * total + total * out_cols + rows * members * out_cols),
            transcendentals=per_dev * tokens * tokens,
        ),
    )(head_class, kv_count, kv_blocks[0].transpose(1, 2, 0), queries[0], keys[0], values[0], weight)
    return result[None]


def solution(mesh):
    placed = (
        P("pipe", "seq", None),
        P("pipe", "seq", None),
        P("pipe", "seq", None),
        P("pipe", None, "seq"),
        P("pipe", None),
        P("pipe", None, None, None),
        P("pipe", None),
    )
    return jax.shard_map(
        functools.partial(shards, mesh.shape["pipe"]),
        mesh=mesh, in_specs=placed, out_specs=P("pipe", "seq", None), check_vma=False,
    )
```

```python
import functools

import jax
import jax.numpy as jnp
from jax import lax
from jax.experimental import pallas as pl
from jax.experimental.pallas import tpu as pltpu
from jax.sharding import PartitionSpec as P

FRAMES = 4
BLOCK = 64
MASKED = 131072.0
LOG2E = 1.4426950408889634
TILE = 256
AHEAD = 2
MESH = pl.DeviceIdType.MESH


def kernel(
    members, per_dev, stages,
    classes, counts, lists, queries, keys, values, weight,
    out,
    qbuf, kbuf, vbuf, ebuf, bbuf, abuf, wboth, cown, csend, crecv, osend, obuf,
    qkv_send, qkv_recv, qkv_local, w_sems, w_local, up_send, down_send, side_send, a_recv,
    c_send, c_recv, o_send, o_recv,
):
    stage = lax.axis_index("pipe")
    me = lax.axis_index("seq")
    half = lax.rem(me, 2)
    col = me // 2
    side = lax.rem(col, 2)
    level = col // 2
    levels = members // 4
    cols = members // 2
    partner = me + 1 - 2 * half
    across = me + 2 - 4 * side
    following = lax.rem(stage + 1, stages)
    preceding = lax.rem(stage + stages - 1, stages)
    rows, width = queries.shape[0], kbuf.shape[-1]
    tokens = rows * members
    depth = per_dev * width
    out_cols = weight.shape[0]
    tile = TILE
    chunks = tokens // tile
    group = tile // rows
    tensors = ((queries, qbuf), (keys, kbuf), (values, vbuf))

    def block_at(chunk, place):
        return place * chunks + lax.rem(chunk + place, chunks)

    barrier = pltpu.get_barrier_semaphore()

    def greet(r, carry):
        pl.semaphore_signal(
            barrier, inc=1, device_id={"seq": lax.rem(me + r, members)}, device_id_type=MESH
        )
        return carry

    def greet_preceding(r, carry):
        pl.semaphore_signal(barrier, inc=1, device_id=(preceding, r), device_id_type=MESH)
        return carry

    lax.fori_loop(1, members, greet, 0)
    lax.fori_loop(0, members, greet_preceding, 0)

    def head_columns(owner, slot):
        return pl.ds(pl.multiple_of((owner * per_dev + slot) * width, width), width)

    my_place = me // chunks
    my_chunk = lax.rem(lax.rem(me, chunks) + chunks * group - my_place, chunks)
    mine = pl.ds(pl.multiple_of((my_chunk * group + my_place) * rows, rows), rows)
    own_copies = []
    for slot in range(per_dev):
        for which, (source, landing) in enumerate(tensors):
            copy = pltpu.make_async_copy(
                source.at[:, head_columns(me, slot)],
                landing.at[slot, mine],
                qkv_local.at[slot, which],
            )
            copy.start()
            own_copies.append(copy)
    pl.semaphore_wait(barrier, 2 * members - 1)

    for slot in range(per_dev):

        def send(r, carry):
            peer = lax.rem(me + r, members)
            for which, (source, landing) in enumerate(tensors):
                pltpu.make_async_remote_copy(
                    src_ref=source.at[:, head_columns(peer, slot)],
                    dst_ref=landing.at[slot, mine],
                    send_sem=qkv_send.at[slot, which],
                    recv_sem=qkv_recv.at[slot, which],
                    device_id={"seq": peer},
                    device_id_type=MESH,
                ).start()
            return carry

        lax.fori_loop(1, members, send, 0)

    def weight_columns(column, which_half):
        return pl.ds(pl.multiple_of((2 * column + which_half) * depth, depth), depth)

    def own_weight(column, carry):
        pltpu.make_async_copy(
            weight.at[:, weight_columns(column, half)],
            wboth.at[pl.ds(0, out_cols), pl.ds(pl.multiple_of(column * depth, depth), depth)],
            w_local,
        ).start()
        return carry

    lax.fori_loop(0, cols, own_weight, 0)

    nblock = lists.shape[0]
    place = lax.broadcasted_iota(jnp.int32, (tokens, width), 0)
    lane = lax.broadcasted_iota(jnp.int32, (tokens, width), 1)
    token = block_at(place // tile, lax.rem(place, tile) // rows) * rows + lax.rem(place, rows)
    spatial = token // BLOCK
    temporal = lax.rem(token, tokens // FRAMES) // (BLOCK // FRAMES)
    every = lists[...].astype(jnp.float32)
    head_lane = lax.broadcasted_iota(jnp.int32, every.shape, 2)
    entry = lax.broadcasted_iota(jnp.int32, every.shape[:2] + (width,), 1)
    listed_lane = lax.broadcasted_iota(jnp.int32, entry.shape, 2).astype(jnp.float32)
    for slot in range(per_dev):
        head = me * per_dev + slot
        block_of = jnp.where(classes[0, head] == 1, temporal, spatial)
        member = jnp.where(block_of == lane, 1.0, 0.0).astype(jnp.bfloat16)
        ebuf[slot] = member
        entries = jnp.sum(jnp.where(head_lane == head, every, 0.0), axis=2, keepdims=True)
        usable = jnp.where(entry < counts[0, head], 0.0, -MASKED)
        offset = jnp.max(jnp.where(entries == listed_lane, usable, -MASKED), axis=1)
        offset = jnp.concatenate(
            [offset, jnp.zeros((width - nblock, width), jnp.float32)], axis=0
        ).astype(jnp.bfloat16)
        bbuf[slot] = lax.dot_general(
            member, offset, (((1,), (1,)), ((), ())), preferred_element_type=jnp.float32
        ).astype(jnp.bfloat16)
    for copy in own_copies:
        copy.wait()

    scale = LOG2E * width ** (-0.5)
    others = pl.ds(0, tokens - rows)

    def chunk_rows(chunk):
        return pl.ds(pl.multiple_of(chunk * tile, tile), tile)

    def piece_copy(source_level, slot, chunk, target, sems):
        column = 2 * source_level + side
        piece = abuf.at[column, slot, chunk_rows(chunk)]
        return pltpu.make_async_remote_copy(
            src_ref=piece,
            dst_ref=piece,
            send_sem=sems.at[slot, chunk, source_level],
            recv_sem=a_recv.at[column, slot, chunk],
            device_id={"seq": target},
            device_id_type=MESH,
        )

    def received(column, slot, chunk):
        piece = abuf.at[column, slot, chunk_rows(chunk)]
        pltpu.make_async_copy(piece, piece, a_recv.at[column, slot, chunk]).wait()

    def send_up(source_level, slot, chunk):
        @pl.when(level + 1 < levels)
        def _():
            piece_copy(source_level, slot, chunk, me + 4, up_send).start()

    def send_down(source_level, slot, chunk):
        @pl.when(level >= 1)
        def _():
            piece_copy(source_level, slot, chunk, me - 4, down_send).start()

    def send_side(source_level, slot, chunk):
        piece_copy(source_level, slot, chunk, across, side_send).start()

    def attend(slot, then):
        for which, (source, landing) in enumerate(tensors):
            span = landing.at[slot, others]
            pltpu.make_async_copy(span, span, qkv_recv.at[slot, which]).wait()

        def step(chunk, carry):
            here = chunk_rows(chunk)
            wide_query = jnp.concatenate([qbuf[slot, here], ebuf[slot, here]], axis=1)
            wide_key = jnp.concatenate([kbuf[slot], bbuf[slot]], axis=1)
            scores = lax.dot_general(
                wide_query, wide_key, (((1,), (1,)), ((), ())), preferred_element_type=jnp.float32
            )
            top = jnp.max(scores, axis=1, keepdims=True)
            probs = jnp.exp2((scores - top) * scale).astype(jnp.bfloat16)
            wide_value = jnp.concatenate(
                [vbuf[slot], jnp.ones((tokens, width), jnp.bfloat16)], axis=1
            )
            sums = jnp.dot(probs, wide_value, preferred_element_type=jnp.float32)
            abuf[col, slot, here] = (sums[:, :width] / sums[:, width:]).astype(jnp.bfloat16)
            send_up(level, slot, chunk)
            send_down(level, slot, chunk)
            send_side(level, slot, chunk)
            if then is not None:
                then(chunk)
            return carry

        lax.fori_loop(0, chunks, step, 0)

    def relay(slot, chunk, first, last):
        def hop(t, carry):
            below = level - 1 - t
            above = level + 1 + t

            @pl.when(below >= 0)
            def _():
                received(2 * below + side, slot, chunk)
                send_up(below, slot, chunk)
                send_side(below, slot, chunk)

            @pl.when(above < levels)
            def _():
                received(2 * above + side, slot, chunk)
                send_down(above, slot, chunk)
                send_side(above, slot, chunk)

            return carry

        lax.fori_loop(first, last, hop, 0)

    def relay_all(slot, first, last):
        def step(chunk, carry):
            relay(slot, chunk, first, last)
            return carry

        lax.fori_loop(0, chunks, step, 0)

    weight_span = wboth.at[pl.ds(out_cols, out_cols)]
    for slot in range(per_dev):
        before = None
        if slot > 0:
            before = functools.partial(relay, slot - 1, first=1, last=2)
        attend(slot, before)
        if slot == 0:

            def swap_weight(column, carry):
                pltpu.make_async_remote_copy(
                    src_ref=weight.at[:, weight_columns(column, 1 - half)],
                    dst_ref=wboth.at[
                        pl.ds(out_cols, out_cols),
                        pl.ds(pl.multiple_of(column * depth, depth), depth),
                    ],
                    send_sem=w_sems.at[0],
                    recv_sem=w_sems.at[1],
                    device_id={"seq": partner},
                    device_id_type=MESH,
                ).start()
                return carry

            lax.fori_loop(0, cols, swap_weight, 0)
        else:
            relay_all(slot - 1, 2, levels - 1)
        if slot < per_dev - 1:
            relay_all(slot, 0, 1)

    def relay_last(chunk, carry):
        relay(per_dev - 1, chunk, 0, levels - 1)
        return carry

    lax.fori_loop(0, AHEAD, relay_last, 0)
    weight_own = wboth.at[pl.ds(0, out_cols)]
    pltpu.make_async_copy(weight_own, weight_own, w_local).wait()
    pltpu.make_async_copy(weight_span, weight_span, w_sems.at[1]).wait()

    def chunk_copy(chunk):
        here = chunk_rows(chunk)
        return pltpu.make_async_remote_copy(
            src_ref=csend.at[here],
            dst_ref=crecv.at[here],
            send_sem=c_send.at[chunk],
            recv_sem=c_recv.at[chunk],
            device_id={"seq": partner},
            device_id_type=MESH,
        )

    def row_copy(chunk, q):
        start = pl.multiple_of((chunk * group + q) * rows, rows)
        return pltpu.make_async_remote_copy(
            src_ref=osend.at[pl.ds(start, rows)],
            dst_ref=obuf.at[me],
            send_sem=o_send.at[chunk * group + q],
            recv_sem=o_recv.at[me],
            device_id=(following, block_at(chunk, q)),
            device_id_type=MESH,
        )

    def hand(chunk):
        here = chunk_rows(chunk)
        chunk_copy(chunk).wait_recv()
        osend[here] = (cown[here] + crecv[here].astype(jnp.float32)).astype(jnp.bfloat16)
        for q in range(group):
            row_copy(chunk, q).start()

    def finish(chunk, carry):
        here = chunk_rows(chunk)

        @pl.when(chunk + AHEAD < chunks)
        def _():
            relay_last(chunk + AHEAD, 0)

        def from_side(source_level, inner):
            for slot in range(per_dev):
                received(2 * source_level + 1 - side, slot, chunk)
            return inner

        lax.fori_loop(0, levels, from_side, 0)
        piece = jnp.concatenate(
            [abuf[column, slot, here] for column in range(cols) for slot in range(per_dev)], axis=1
        )
        shares = lax.dot_general(
            piece, wboth[...], (((1,), (1,)), ((), ())), preferred_element_type=jnp.float32
        )
        csend[here] = shares[:, out_cols:].astype(jnp.bfloat16)
        chunk_copy(chunk).start()
        cown[here] = shares[:, :out_cols]

        @pl.when(chunk >= 1)
        def _():
            hand(chunk - 1)

        return carry

    lax.fori_loop(0, chunks, finish, 0)
    hand(chunks - 1)

    for slot in range(per_dev):
        for which, (source, landing) in enumerate(tensors):
            span = landing.at[slot, others]
            pltpu.make_async_copy(span, span, qkv_send.at[slot, which]).wait()
    pltpu.make_async_copy(weight_span, weight_span, w_sems.at[0]).wait()

    def left(chunk, carry):
        for slot in range(per_dev):

            def from_level(source_level, inner):
                @pl.when((level + 1 < levels) & (source_level <= level))
                def _():
                    piece_copy(source_level, slot, chunk, across, up_send).wait_send()

                @pl.when((level >= 1) & (source_level >= level))
                def _():
                    piece_copy(source_level, slot, chunk, across, down_send).wait_send()

                piece_copy(source_level, slot, chunk, across, side_send).wait_send()
                return inner

            lax.fori_loop(0, levels, from_level, 0)
        chunk_copy(chunk).wait_send()
        for q in range(group):
            row_copy(chunk, q).wait_send()
        return carry

    lax.fori_loop(0, chunks, left, 0)

    def arrived(source, carry):
        pltpu.make_async_copy(obuf.at[source], obuf.at[source], o_recv.at[source]).wait()
        return carry

    lax.fori_loop(0, members, arrived, 0)
    pair = 2 * out_cols
    for i in range(members // 2):
        out[:, i * pair : (i + 1) * pair] = jnp.concatenate([obuf[2 * i], obuf[2 * i + 1]], axis=1)


def shards(stages, queries, keys, values, out_weight, head_class, kv_blocks, kv_count):
    members = lax.axis_size("seq")
    heads = head_class.shape[1]
    per_dev = heads // members
    rows, total = queries.shape[1:]
    width = total // heads
    tokens = rows * members
    out_cols = out_weight.shape[2]
    cols = members // 2
    depth = per_dev * width
    weight = out_weight[0].T
    bf16, f32 = jnp.bfloat16, jnp.float32
    dma = pltpu.SemaphoreType.DMA
    vmem = pl.BlockSpec(memory_space=pltpu.VMEM)
    smem = pl.BlockSpec(memory_space=pltpu.SMEM)
    hbm = pl.BlockSpec(memory_space=pl.ANY)
    head_buffer = pltpu.VMEM((per_dev, tokens, width), bf16)
    levels = members // 4
    chunks = tokens // TILE
    result = pl.pallas_call(
        functools.partial(kernel, members, per_dev, stages),
        out_shape=jax.ShapeDtypeStruct((rows, members * out_cols), bf16),
        in_specs=[smem, smem, vmem, hbm, hbm, hbm, hbm],
        out_specs=vmem,
        scratch_shapes=[
            head_buffer, head_buffer, head_buffer, head_buffer, head_buffer,
            pltpu.VMEM((cols, per_dev, tokens, width), bf16),
            pltpu.VMEM((2 * out_cols, cols * depth), bf16),
            pltpu.VMEM((tokens, out_cols), f32),
            pltpu.VMEM((tokens, out_cols), bf16),
            pltpu.VMEM((tokens, out_cols), bf16),
            pltpu.VMEM((tokens, out_cols), bf16),
            pltpu.VMEM((members, rows, out_cols), bf16),
            dma((per_dev, 3)), dma((per_dev, 3)), dma((per_dev, 3)),
            dma((2,)), dma,
            dma((per_dev, chunks, levels)), dma((per_dev, chunks, levels)),
            dma((per_dev, chunks, levels)), dma((cols, per_dev, chunks)),
            dma((chunks,)), dma((chunks,)),
            dma((members,)), dma((members,)),
        ],
        compiler_params=pltpu.CompilerParams(
            collective_id=0, has_side_effects=True, vmem_limit_bytes=60 * 1024 * 1024
        ),
        cost_estimate=pl.CostEstimate(
            flops=4 * tokens * tokens * depth + 2 * tokens * total * out_cols,
            bytes_accessed=2 * (3 * rows * total + total * out_cols + rows * members * out_cols),
            transcendentals=per_dev * tokens * tokens,
        ),
    )(head_class, kv_count, kv_blocks[0].transpose(1, 2, 0), queries[0], keys[0], values[0], weight)
    return result[None]


def solution(mesh):
    placed = (
        P("pipe", "seq", None),
        P("pipe", "seq", None),
        P("pipe", "seq", None),
        P("pipe", None, "seq"),
        P("pipe", None),
        P("pipe", None, None, None),
        P("pipe", None),
    )
    return jax.shard_map(
        functools.partial(shards, mesh.shape["pipe"]),
        mesh=mesh, in_specs=placed, out_specs=P("pipe", "seq", None), check_vma=False,
    )
```

```python
import functools

import jax
import jax.numpy as jnp
from jax import lax
from jax.experimental import pallas as pl
from jax.experimental.pallas import tpu as pltpu
from jax.sharding import PartitionSpec as P

FRAMES = 4
BLOCK = 64
MASKED = 131072.0
LOG2E = 1.4426950408889634
TILE = 256
AHEAD = 3
MESH = pl.DeviceIdType.MESH


def kernel(
    members, per_dev, stages,
    classes, counts, lists, queries, keys, values, weight,
    out,
    qbuf, kbuf, vbuf, ebuf, bbuf, abuf, wboth, cown, csend, crecv, osend, obuf,
    qkv_send, qkv_recv, qkv_local, w_sems, w_local, up_send, down_send, side_send, a_recv,
    c_send, c_recv, o_send, o_recv,
):
    stage = lax.axis_index("pipe")
    me = lax.axis_index("seq")
    half = lax.rem(me, 2)
    col = me // 2
    side = lax.rem(col, 2)
    level = col // 2
    levels = members // 4
    cols = members // 2
    partner = me + 1 - 2 * half
    across = me + 2 - 4 * side
    following = lax.rem(stage + 1, stages)
    preceding = lax.rem(stage + stages - 1, stages)
    rows, width = queries.shape[0], kbuf.shape[-1]
    tokens = rows * members
    depth = per_dev * width
    out_cols = weight.shape[0]
    tile = TILE
    chunks = tokens // tile
    group = tile // rows
    tensors = ((queries, qbuf), (keys, kbuf), (values, vbuf))

    def block_at(chunk, place):
        return place * chunks + lax.rem(chunk + place, chunks)

    barrier = pltpu.get_barrier_semaphore()

    def greet(r, carry):
        pl.semaphore_signal(
            barrier, inc=1, device_id={"seq": lax.rem(me + r, members)}, device_id_type=MESH
        )
        return carry

    def greet_preceding(r, carry):
        pl.semaphore_signal(barrier, inc=1, device_id=(preceding, r), device_id_type=MESH)
        return carry

    lax.fori_loop(1, members, greet, 0)
    lax.fori_loop(0, members, greet_preceding, 0)

    def head_columns(owner, slot):
        return pl.ds(pl.multiple_of((owner * per_dev + slot) * width, width), width)

    my_place = me // chunks
    my_chunk = lax.rem(lax.rem(me, chunks) + chunks * group - my_place, chunks)
    mine = pl.ds(pl.multiple_of((my_chunk * group + my_place) * rows, rows), rows)
    own_copies = []
    for slot in range(per_dev):
        for which, (source, landing) in enumerate(tensors):
            copy = pltpu.make_async_copy(
                source.at[:, head_columns(me, slot)],
                landing.at[slot, mine],
                qkv_local.at[slot, which],
            )
            copy.start()
            own_copies.append(copy)
    pl.semaphore_wait(barrier, 2 * members - 1)

    for slot in range(per_dev):

        def send(r, carry):
            peer = lax.rem(me + r * (members // 2 - 1), members)
            for which, (source, landing) in enumerate(tensors):
                pltpu.make_async_remote_copy(
                    src_ref=source.at[:, head_columns(peer, slot)],
                    dst_ref=landing.at[slot, mine],
                    send_sem=qkv_send.at[slot, which],
                    recv_sem=qkv_recv.at[slot, which],
                    device_id={"seq": peer},
                    device_id_type=MESH,
                ).start()
            return carry

        lax.fori_loop(1, members, send, 0)

    def weight_columns(column, which_half):
        return pl.ds(pl.multiple_of((2 * column + which_half) * depth, depth), depth)

    def own_weight(column, carry):
        pltpu.make_async_copy(
            weight.at[:, weight_columns(column, half)],
            wboth.at[pl.ds(0, out_cols), pl.ds(pl.multiple_of(column * depth, depth), depth)],
            w_local,
        ).start()
        return carry

    lax.fori_loop(0, cols, own_weight, 0)

    nblock = lists.shape[0]
    place = lax.broadcasted_iota(jnp.int32, (tokens, width), 0)
    lane = lax.broadcasted_iota(jnp.int32, (tokens, width), 1)
    token = block_at(place // tile, lax.rem(place, tile) // rows) * rows + lax.rem(place, rows)
    spatial = token // BLOCK
    temporal = lax.rem(token, tokens // FRAMES) // (BLOCK // FRAMES)
    every = lists[...].astype(jnp.float32)
    head_lane = lax.broadcasted_iota(jnp.int32, every.shape, 2)
    entry = lax.broadcasted_iota(jnp.int32, every.shape[:2] + (width,), 1)
    listed_lane = lax.broadcasted_iota(jnp.int32, entry.shape, 2).astype(jnp.float32)
    for slot in range(per_dev):
        head = me * per_dev + slot
        block_of = jnp.where(classes[0, head] == 1, temporal, spatial)
        member = jnp.where(block_of == lane, 1.0, 0.0).astype(jnp.bfloat16)
        ebuf[slot] = member
        entries = jnp.sum(jnp.where(head_lane == head, every, 0.0), axis=2, keepdims=True)
        usable = jnp.where(entry < counts[0, head], 0.0, -MASKED)
        offset = jnp.max(jnp.where(entries == listed_lane, usable, -MASKED), axis=1)
        offset = jnp.concatenate(
            [offset, jnp.zeros((width - nblock, width), jnp.float32)], axis=0
        ).astype(jnp.bfloat16)
        bbuf[slot] = lax.dot_general(
            member, offset, (((1,), (1,)), ((), ())), preferred_element_type=jnp.float32
        ).astype(jnp.bfloat16)
    for copy in own_copies:
        copy.wait()

    scale = LOG2E * width ** (-0.5)
    others = pl.ds(0, tokens - rows)

    def chunk_rows(chunk):
        return pl.ds(pl.multiple_of(chunk * tile, tile), tile)

    def piece_copy(source_level, slot, chunk, target, sems):
        column = 2 * source_level + side
        piece = abuf.at[column, slot, chunk_rows(chunk)]
        return pltpu.make_async_remote_copy(
            src_ref=piece,
            dst_ref=piece,
            send_sem=sems.at[slot, chunk, source_level],
            recv_sem=a_recv.at[column, slot, chunk],
            device_id={"seq": target},
            device_id_type=MESH,
        )

    def received(column, slot, chunk):
        piece = abuf.at[column, slot, chunk_rows(chunk)]
        pltpu.make_async_copy(piece, piece, a_recv.at[column, slot, chunk]).wait()

    def send_up(source_level, slot, chunk):
        @pl.when(level + 1 < levels)
        def _():
            piece_copy(source_level, slot, chunk, me + 4, up_send).start()

    def send_down(source_level, slot, chunk):
        @pl.when(level >= 1)
        def _():
            piece_copy(source_level, slot, chunk, me - 4, down_send).start()

    def send_side(source_level, slot, chunk):
        piece_copy(source_level, slot, chunk, across, side_send).start()

    def attend(slot, then):
        for which, (source, landing) in enumerate(tensors):
            span = landing.at[slot, others]
            pltpu.make_async_copy(span, span, qkv_recv.at[slot, which]).wait()

        def step(chunk, carry):
            here = chunk_rows(chunk)
            wide_query = jnp.concatenate([qbuf[slot, here], ebuf[slot, here]], axis=1)
            wide_key = jnp.concatenate([kbuf[slot], bbuf[slot]], axis=1)
            scores = lax.dot_general(
                wide_query, wide_key, (((1,), (1,)), ((), ())), preferred_element_type=jnp.float32
            )
            top = jnp.max(scores, axis=1, keepdims=True)
            probs = jnp.exp2((scores - top) * scale).astype(jnp.bfloat16)
            wide_value = jnp.concatenate(
                [vbuf[slot], jnp.ones((tokens, width), jnp.bfloat16)], axis=1
            )
            sums = jnp.dot(probs, wide_value, preferred_element_type=jnp.float32)
            abuf[col, slot, here] = (sums[:, :width] / sums[:, width:]).astype(jnp.bfloat16)
            send_up(level, slot, chunk)
            send_down(level, slot, chunk)
            send_side(level, slot, chunk)
            if then is not None:
                then(chunk)
            return carry

        lax.fori_loop(0, chunks, step, 0)

    def relay(slot, chunk, first, last):
        def hop(t, carry):
            below = level - 1 - t
            above = level + 1 + t

            @pl.when(below >= 0)
            def _():
                received(2 * below + side, slot, chunk)
                send_up(below, slot, chunk)
                send_side(below, slot, chunk)

            @pl.when(above < levels)
            def _():
                received(2 * above + side, slot, chunk)
                send_down(above, slot, chunk)
                send_side(above, slot, chunk)

            return carry

        lax.fori_loop(first, last, hop, 0)

    def relay_all(slot, first, last):
        def step(chunk, carry):
            relay(slot, chunk, first, last)
            return carry

        lax.fori_loop(0, chunks, step, 0)

    weight_span = wboth.at[pl.ds(out_cols, out_cols)]
    for slot in range(per_dev):
        before = None
        if slot > 0:
            before = functools.partial(relay, slot - 1, first=1, last=2)
        attend(slot, before)
        if slot == 0:

            def swap_weight(column, carry):
                pltpu.make_async_remote_copy(
                    src_ref=weight.at[:, weight_columns(column, 1 - half)],
                    dst_ref=wboth.at[
                        pl.ds(out_cols, out_cols),
                        pl.ds(pl.multiple_of(column * depth, depth), depth),
                    ],
                    send_sem=w_sems.at[0],
                    recv_sem=w_sems.at[1],
                    device_id={"seq": partner},
                    device_id_type=MESH,
                ).start()
                return carry

            lax.fori_loop(0, cols, swap_weight, 0)
        else:
            relay_all(slot - 1, 2, levels - 1)
        if slot < per_dev - 1:
            relay_all(slot, 0, 1)

    def relay_last(chunk, carry):
        relay(per_dev - 1, chunk, 0, levels - 1)
        return carry

    lax.fori_loop(0, AHEAD, relay_last, 0)
    weight_own = wboth.at[pl.ds(0, out_cols)]
    pltpu.make_async_copy(weight_own, weight_own, w_local).wait()
    pltpu.make_async_copy(weight_span, weight_span, w_sems.at[1]).wait()

    def chunk_copy(chunk):
        here = chunk_rows(chunk)
        return pltpu.make_async_remote_copy(
            src_ref=csend.at[here],
            dst_ref=crecv.at[here],
            send_sem=c_send.at[chunk],
            recv_sem=c_recv.at[chunk],
            device_id={"seq": partner},
            device_id_type=MESH,
        )

    def row_copy(chunk, q):
        start = pl.multiple_of((chunk * group + q) * rows, rows)
        return pltpu.make_async_remote_copy(
            src_ref=osend.at[pl.ds(start, rows)],
            dst_ref=obuf.at[me],
            send_sem=o_send.at[chunk * group + q],
            recv_sem=o_recv.at[me],
            device_id=(following, block_at(chunk, q)),
            device_id_type=MESH,
        )

    def hand(chunk):
        here = chunk_rows(chunk)
        chunk_copy(chunk).wait_recv()
        osend[here] = (cown[here] + crecv[here].astype(jnp.float32)).astype(jnp.bfloat16)
        for q in range(group):
            row_copy(chunk, lax.rem(level + q, group)).start()

    def finish(chunk, carry):
        here = chunk_rows(chunk)

        @pl.when(chunk + AHEAD < chunks)
        def _():
            relay_last(chunk + AHEAD, 0)

        def from_side(source_level, inner):
            for slot in range(per_dev):
                received(2 * source_level + 1 - side, slot, chunk)
            return inner

        lax.fori_loop(0, levels, from_side, 0)
        piece = jnp.concatenate(
            [abuf[column, slot, here] for column in range(cols) for slot in range(per_dev)], axis=1
        )
        shares = lax.dot_general(
            piece, wboth[...], (((1,), (1,)), ((), ())), preferred_element_type=jnp.float32
        )
        csend[here] = shares[:, out_cols:].astype(jnp.bfloat16)
        chunk_copy(chunk).start()
        cown[here] = shares[:, :out_cols]

        @pl.when(chunk >= 1)
        def _():
            hand(chunk - 1)

        return carry

    lax.fori_loop(0, chunks, finish, 0)
    hand(chunks - 1)

    for slot in range(per_dev):
        for which, (source, landing) in enumerate(tensors):
            span = landing.at[slot, others]
            pltpu.make_async_copy(span, span, qkv_send.at[slot, which]).wait()
    pltpu.make_async_copy(weight_span, weight_span, w_sems.at[0]).wait()

    def left(chunk, carry):
        for slot in range(per_dev):

            def from_level(source_level, inner):
                @pl.when((level + 1 < levels) & (source_level <= level))
                def _():
                    piece_copy(source_level, slot, chunk, across, up_send).wait_send()

                @pl.when((level >= 1) & (source_level >= level))
                def _():
                    piece_copy(source_level, slot, chunk, across, down_send).wait_send()

                piece_copy(source_level, slot, chunk, across, side_send).wait_send()
                return inner

            lax.fori_loop(0, levels, from_level, 0)
        chunk_copy(chunk).wait_send()
        for q in range(group):
            row_copy(chunk, q).wait_send()
        return carry

    lax.fori_loop(0, chunks, left, 0)

    def arrived(source, carry):
        pltpu.make_async_copy(obuf.at[source], obuf.at[source], o_recv.at[source]).wait()
        return carry

    lax.fori_loop(0, members, arrived, 0)
    pair = 2 * out_cols
    for i in range(members // 2):
        out[:, i * pair : (i + 1) * pair] = jnp.concatenate([obuf[2 * i], obuf[2 * i + 1]], axis=1)


def shards(stages, queries, keys, values, out_weight, head_class, kv_blocks, kv_count):
    members = lax.axis_size("seq")
    heads = head_class.shape[1]
    per_dev = heads // members
    rows, total = queries.shape[1:]
    width = total // heads
    tokens = rows * members
    out_cols = out_weight.shape[2]
    cols = members // 2
    depth = per_dev * width
    weight = out_weight[0].T
    bf16, f32 = jnp.bfloat16, jnp.float32
    dma = pltpu.SemaphoreType.DMA
    vmem = pl.BlockSpec(memory_space=pltpu.VMEM)
    smem = pl.BlockSpec(memory_space=pltpu.SMEM)
    hbm = pl.BlockSpec(memory_space=pl.ANY)
    head_buffer = pltpu.VMEM((per_dev, tokens, width), bf16)
    levels = members // 4
    chunks = tokens // TILE
    result = pl.pallas_call(
        functools.partial(kernel, members, per_dev, stages),
        out_shape=jax.ShapeDtypeStruct((rows, members * out_cols), bf16),
        in_specs=[smem, smem, vmem, hbm, hbm, hbm, hbm],
        out_specs=vmem,
        scratch_shapes=[
            head_buffer, head_buffer, head_buffer, head_buffer, head_buffer,
            pltpu.VMEM((cols, per_dev, tokens, width), bf16),
            pltpu.VMEM((2 * out_cols, cols * depth), bf16),
            pltpu.VMEM((tokens, out_cols), f32),
            pltpu.VMEM((tokens, out_cols), bf16),
            pltpu.VMEM((tokens, out_cols), bf16),
            pltpu.VMEM((tokens, out_cols), bf16),
            pltpu.VMEM((members, rows, out_cols), bf16),
            dma((per_dev, 3)), dma((per_dev, 3)), dma((per_dev, 3)),
            dma((2,)), dma,
            dma((per_dev, chunks, levels)), dma((per_dev, chunks, levels)),
            dma((per_dev, chunks, levels)), dma((cols, per_dev, chunks)),
            dma((chunks,)), dma((chunks,)),
            dma((members,)), dma((members,)),
        ],
        compiler_params=pltpu.CompilerParams(
            collective_id=0, has_side_effects=True, vmem_limit_bytes=60 * 1024 * 1024
        ),
        cost_estimate=pl.CostEstimate(
            flops=4 * tokens * tokens * depth + 2 * tokens * total * out_cols,
            bytes_accessed=2 * (3 * rows * total + total * out_cols + rows * members * out_cols),
            transcendentals=per_dev * tokens * tokens,
        ),
    )(head_class, kv_count, kv_blocks[0].transpose(1, 2, 0), queries[0], keys[0], values[0], weight)
    return result[None]


def solution(mesh):
    placed = (
        P("pipe", "seq", None),
        P("pipe", "seq", None),
        P("pipe", "seq", None),
        P("pipe", None, "seq"),
        P("pipe", None),
        P("pipe", None, None, None),
        P("pipe", None),
    )
    return jax.shard_map(
        functools.partial(shards, mesh.shape["pipe"]),
        mesh=mesh, in_specs=placed, out_specs=P("pipe", "seq", None), check_vma=False,
    )
```

```python
import functools

import jax
import jax.numpy as jnp
from jax import lax
from jax.experimental import pallas as pl
from jax.experimental.pallas import tpu as pltpu
from jax.sharding import PartitionSpec as P

FRAMES = 4
BLOCK = 64
MASKED = 131072.0
LOG2E = 1.4426950408889634
TILE = 256
AHEAD = 3
MESH = pl.DeviceIdType.MESH


def kernel(
    members, per_dev, stages,
    classes, counts, lists, queries, keys, values, weight,
    out,
    qbuf, kbuf, vbuf, ebuf, bbuf, abuf, wboth, cown, csend, crecv, osend, obuf,
    qkv_send, qkv_recv, qkv_local, w_sems, w_local, up_send, down_send, side_send, a_recv,
    c_send, c_recv, o_send, o_recv,
):
    stage = lax.axis_index("pipe")
    me = lax.axis_index("seq")
    half = lax.rem(me, 2)
    col = me // 2
    side = lax.rem(col, 2)
    level = col // 2
    levels = members // 4
    cols = members // 2
    partner = me + 1 - 2 * half
    across = me + 2 - 4 * side
    following = lax.rem(stage + 1, stages)
    preceding = lax.rem(stage + stages - 1, stages)
    rows, width = queries.shape[0], kbuf.shape[-1]
    tokens = rows * members
    depth = per_dev * width
    out_cols = weight.shape[0]
    tile = TILE
    chunks = tokens // tile
    group = tile // rows
    tensors = ((queries, qbuf), (keys, kbuf), (values, vbuf))

    def block_at(chunk, place):
        return place * chunks + lax.rem(chunk + place, chunks)

    barrier = pltpu.get_barrier_semaphore()

    def greet(r, carry):
        pl.semaphore_signal(
            barrier, inc=1, device_id={"seq": lax.rem(me + r, members)}, device_id_type=MESH
        )
        return carry

    def greet_preceding(r, carry):
        pl.semaphore_signal(barrier, inc=1, device_id=(preceding, r), device_id_type=MESH)
        return carry

    lax.fori_loop(1, members, greet, 0)
    lax.fori_loop(0, members, greet_preceding, 0)

    def head_columns(owner, slot):
        return pl.ds(pl.multiple_of((owner * per_dev + slot) * width, width), width)

    my_place = me // chunks
    my_chunk = lax.rem(lax.rem(me, chunks) + chunks * group - my_place, chunks)
    mine = pl.ds(pl.multiple_of((my_chunk * group + my_place) * rows, rows), rows)
    own_copies = []
    for slot in range(per_dev):
        for which, (source, landing) in enumerate(tensors):
            copy = pltpu.make_async_copy(
                source.at[:, head_columns(me, slot)],
                landing.at[slot, mine],
                qkv_local.at[slot, which],
            )
            copy.start()
            own_copies.append(copy)
    pl.semaphore_wait(barrier, 2 * members - 1)

    for slot in range(per_dev):

        def send(r, carry):
            peer = lax.rem(me + r * (members // 2 - 1), members)
            for which, (source, landing) in enumerate(tensors):
                pltpu.make_async_remote_copy(
                    src_ref=source.at[:, head_columns(peer, slot)],
                    dst_ref=landing.at[slot, mine],
                    send_sem=qkv_send.at[slot, which],
                    recv_sem=qkv_recv.at[slot, which],
                    device_id={"seq": peer},
                    device_id_type=MESH,
                ).start()
            return carry

        lax.fori_loop(1, members, send, 0)

    def weight_columns(column, which_half):
        return pl.ds(pl.multiple_of((2 * column + which_half) * depth, depth), depth)

    def own_weight(column, carry):
        pltpu.make_async_copy(
            weight.at[:, weight_columns(column, half)],
            wboth.at[pl.ds(0, out_cols), pl.ds(pl.multiple_of(column * depth, depth), depth)],
            w_local,
        ).start()
        return carry

    lax.fori_loop(0, cols, own_weight, 0)

    nblock = lists.shape[0]
    place = lax.broadcasted_iota(jnp.int32, (tokens, width), 0)
    lane = lax.broadcasted_iota(jnp.int32, (tokens, width), 1)
    token = block_at(place // tile, lax.rem(place, tile) // rows) * rows + lax.rem(place, rows)
    spatial = token // BLOCK
    temporal = lax.rem(token, tokens // FRAMES) // (BLOCK // FRAMES)
    every = lists[...].astype(jnp.float32)
    head_lane = lax.broadcasted_iota(jnp.int32, every.shape, 2)
    entry = lax.broadcasted_iota(jnp.int32, every.shape[:2] + (width,), 1)
    listed_lane = lax.broadcasted_iota(jnp.int32, entry.shape, 2).astype(jnp.float32)
    for slot in range(per_dev):
        head = me * per_dev + slot
        block_of = jnp.where(classes[0, head] == 1, temporal, spatial)
        member = jnp.where(block_of == lane, 1.0, 0.0).astype(jnp.bfloat16)
        ebuf[slot] = member
        entries = jnp.sum(jnp.where(head_lane == head, every, 0.0), axis=2, keepdims=True)
        usable = jnp.where(entry < counts[0, head], 0.0, -MASKED)
        offset = jnp.max(jnp.where(entries == listed_lane, usable, -MASKED), axis=1)
        offset = jnp.concatenate(
            [offset, jnp.zeros((width - nblock, width), jnp.float32)], axis=0
        ).astype(jnp.bfloat16)
        bbuf[slot] = lax.dot_general(
            member, offset, (((1,), (1,)), ((), ())), preferred_element_type=jnp.float32
        ).astype(jnp.bfloat16)
    for copy in own_copies:
        copy.wait()

    scale = LOG2E * width ** (-0.5)
    others = pl.ds(0, tokens - rows)

    def chunk_rows(chunk):
        return pl.ds(pl.multiple_of(chunk * tile, tile), tile)

    def piece_copy(source_level, slot, chunk, target, sems):
        column = 2 * source_level + side
        piece = abuf.at[column, slot, chunk_rows(chunk)]
        return pltpu.make_async_remote_copy(
            src_ref=piece,
            dst_ref=piece,
            send_sem=sems.at[slot, chunk, source_level],
            recv_sem=a_recv.at[column, slot, chunk],
            device_id={"seq": target},
            device_id_type=MESH,
        )

    def received(column, slot, chunk):
        piece = abuf.at[column, slot, chunk_rows(chunk)]
        pltpu.make_async_copy(piece, piece, a_recv.at[column, slot, chunk]).wait()

    def send_up(source_level, slot, chunk):
        @pl.when(level + 1 < levels)
        def _():
            piece_copy(source_level, slot, chunk, me + 4, up_send).start()

    def send_down(source_level, slot, chunk):
        @pl.when(level >= 1)
        def _():
            piece_copy(source_level, slot, chunk, me - 4, down_send).start()

    def send_side(source_level, slot, chunk):
        piece_copy(source_level, slot, chunk, across, side_send).start()

    def attend(slot, then):
        for which, (source, landing) in enumerate(tensors):
            span = landing.at[slot, others]
            pltpu.make_async_copy(span, span, qkv_recv.at[slot, which]).wait()

        def step(chunk, carry):
            here = chunk_rows(chunk)
            wide_query = jnp.concatenate([qbuf[slot, here], ebuf[slot, here]], axis=1)
            wide_key = jnp.concatenate([kbuf[slot], bbuf[slot]], axis=1)
            scores = lax.dot_general(
                wide_query, wide_key, (((1,), (1,)), ((), ())), preferred_element_type=jnp.float32
            )
            top = jnp.max(scores, axis=1, keepdims=True)
            probs = jnp.exp2((scores - top) * scale).astype(jnp.bfloat16)
            wide_value = jnp.concatenate(
                [vbuf[slot], jnp.ones((tokens, width), jnp.bfloat16)], axis=1
            )
            sums = jnp.dot(probs, wide_value, preferred_element_type=jnp.float32)
            abuf[col, slot, here] = (sums[:, :width] / sums[:, width:]).astype(jnp.bfloat16)
            send_up(level, slot, chunk)
            send_down(level, slot, chunk)
            send_side(level, slot, chunk)
            then(chunk)
            return carry

        lax.fori_loop(0, chunks, step, 0)

    def relay(slot, chunk, first, last):
        def hop(t, carry):
            below = level - 1 - t
            above = level + 1 + t

            @pl.when(below >= 0)
            def _():
                received(2 * below + side, slot, chunk)
                send_up(below, slot, chunk)
                send_side(below, slot, chunk)

            @pl.when(above < levels)
            def _():
                received(2 * above + side, slot, chunk)
                send_down(above, slot, chunk)
                send_side(above, slot, chunk)

            return carry

        lax.fori_loop(first, last, hop, 0)

    def relay_all(slot, first, last):
        def step(chunk, carry):
            relay(slot, chunk, first, last)
            return carry

        lax.fori_loop(0, chunks, step, 0)

    def swap_weight(column):
        @pl.when(column < cols)
        def _():
            pltpu.make_async_remote_copy(
                src_ref=weight.at[:, weight_columns(column, 1 - half)],
                dst_ref=wboth.at[
                    pl.ds(out_cols, out_cols),
                    pl.ds(pl.multiple_of(column * depth, depth), depth),
                ],
                send_sem=w_sems.at[0],
                recv_sem=w_sems.at[1],
                device_id={"seq": partner},
                device_id_type=MESH,
            ).start()

    weight_span = wboth.at[pl.ds(out_cols, out_cols)]
    for slot in range(per_dev):
        before = swap_weight
        if slot > 0:
            before = functools.partial(relay, slot - 1, first=1, last=2)
        attend(slot, before)
        if slot > 0:
            relay_all(slot - 1, 2, levels - 1)
        if slot < per_dev - 1:

            def first_hop(chunk, carry):
                relay(slot, chunk, 0, 1)
                if slot == 0:
                    swap_weight(chunks + chunk)
                return carry

            lax.fori_loop(0, chunks, first_hop, 0)

    def relay_last(chunk, carry):
        relay(per_dev - 1, chunk, 0, levels - 1)
        return carry

    lax.fori_loop(0, AHEAD, relay_last, 0)
    weight_own = wboth.at[pl.ds(0, out_cols)]
    pltpu.make_async_copy(weight_own, weight_own, w_local).wait()
    pltpu.make_async_copy(weight_span, weight_span, w_sems.at[1]).wait()

    def chunk_copy(chunk):
        here = chunk_rows(chunk)
        return pltpu.make_async_remote_copy(
            src_ref=csend.at[here],
            dst_ref=crecv.at[here],
            send_sem=c_send.at[chunk],
            recv_sem=c_recv.at[chunk],
            device_id={"seq": partner},
            device_id_type=MESH,
        )

    def row_copy(chunk, q):
        start = pl.multiple_of((chunk * group + q) * rows, rows)
        return pltpu.make_async_remote_copy(
            src_ref=osend.at[pl.ds(start, rows)],
            dst_ref=obuf.at[me],
            send_sem=o_send.at[chunk * group + q],
            recv_sem=o_recv.at[me],
            device_id=(following, block_at(chunk, q)),
            device_id_type=MESH,
        )

    def hand(chunk):
        here = chunk_rows(chunk)
        chunk_copy(chunk).wait_recv()
        osend[here] = (cown[here] + crecv[here].astype(jnp.float32)).astype(jnp.bfloat16)
        for q in range(group):
            row_copy(chunk, lax.rem(level + q, group)).start()

    def finish(chunk, carry):
        here = chunk_rows(chunk)

        @pl.when(chunk + AHEAD < chunks)
        def _():
            relay_last(chunk + AHEAD, 0)

        def from_side(source_level, inner):
            for slot in range(per_dev):
                received(2 * source_level + 1 - side, slot, chunk)
            return inner

        lax.fori_loop(0, levels, from_side, 0)
        piece = jnp.concatenate(
            [abuf[column, slot, here] for column in range(cols) for slot in range(per_dev)], axis=1
        )
        shares = lax.dot_general(
            piece, wboth[...], (((1,), (1,)), ((), ())), preferred_element_type=jnp.float32
        )
        csend[here] = shares[:, out_cols:].astype(jnp.bfloat16)
        chunk_copy(chunk).start()
        cown[here] = shares[:, :out_cols]

        @pl.when(chunk >= 1)
        def _():
            hand(chunk - 1)

        return carry

    lax.fori_loop(0, chunks, finish, 0)
    hand(chunks - 1)

    for slot in range(per_dev):
        for which, (source, landing) in enumerate(tensors):
            span = landing.at[slot, others]
            pltpu.make_async_copy(span, span, qkv_send.at[slot, which]).wait()
    pltpu.make_async_copy(weight_span, weight_span, w_sems.at[0]).wait()

    def left(chunk, carry):
        for slot in range(per_dev):

            def from_level(source_level, inner):
                @pl.when((level + 1 < levels) & (source_level <= level))
                def _():
                    piece_copy(source_level, slot, chunk, across, up_send).wait_send()

                @pl.when((level >= 1) & (source_level >= level))
                def _():
                    piece_copy(source_level, slot, chunk, across, down_send).wait_send()

                piece_copy(source_level, slot, chunk, across, side_send).wait_send()
                return inner

            lax.fori_loop(0, levels, from_level, 0)
        chunk_copy(chunk).wait_send()
        for q in range(group):
            row_copy(chunk, q).wait_send()
        return carry

    lax.fori_loop(0, chunks, left, 0)

    def arrived(source, carry):
        pltpu.make_async_copy(obuf.at[source], obuf.at[source], o_recv.at[source]).wait()
        return carry

    lax.fori_loop(0, members, arrived, 0)
    pair = 2 * out_cols
    for i in range(members // 2):
        out[:, i * pair : (i + 1) * pair] = jnp.concatenate([obuf[2 * i], obuf[2 * i + 1]], axis=1)


def shards(stages, queries, keys, values, out_weight, head_class, kv_blocks, kv_count):
    members = lax.axis_size("seq")
    heads = head_class.shape[1]
    per_dev = heads // members
    rows, total = queries.shape[1:]
    width = total // heads
    tokens = rows * members
    out_cols = out_weight.shape[2]
    cols = members // 2
    depth = per_dev * width
    weight = out_weight[0].T
    bf16, f32 = jnp.bfloat16, jnp.float32
    dma = pltpu.SemaphoreType.DMA
    vmem = pl.BlockSpec(memory_space=pltpu.VMEM)
    smem = pl.BlockSpec(memory_space=pltpu.SMEM)
    hbm = pl.BlockSpec(memory_space=pl.ANY)
    head_buffer = pltpu.VMEM((per_dev, tokens, width), bf16)
    levels = members // 4
    chunks = tokens // TILE
    result = pl.pallas_call(
        functools.partial(kernel, members, per_dev, stages),
        out_shape=jax.ShapeDtypeStruct((rows, members * out_cols), bf16),
        in_specs=[smem, smem, vmem, hbm, hbm, hbm, hbm],
        out_specs=vmem,
        scratch_shapes=[
            head_buffer, head_buffer, head_buffer, head_buffer, head_buffer,
            pltpu.VMEM((cols, per_dev, tokens, width), bf16),
            pltpu.VMEM((2 * out_cols, cols * depth), bf16),
            pltpu.VMEM((tokens, out_cols), f32),
            pltpu.VMEM((tokens, out_cols), bf16),
            pltpu.VMEM((tokens, out_cols), bf16),
            pltpu.VMEM((tokens, out_cols), bf16),
            pltpu.VMEM((members, rows, out_cols), bf16),
            dma((per_dev, 3)), dma((per_dev, 3)), dma((per_dev, 3)),
            dma((2,)), dma,
            dma((per_dev, chunks, levels)), dma((per_dev, chunks, levels)),
            dma((per_dev, chunks, levels)), dma((cols, per_dev, chunks)),
            dma((chunks,)), dma((chunks,)),
            dma((members,)), dma((members,)),
        ],
        compiler_params=pltpu.CompilerParams(
            collective_id=0, has_side_effects=True, vmem_limit_bytes=60 * 1024 * 1024
        ),
        cost_estimate=pl.CostEstimate(
            flops=4 * tokens * tokens * depth + 2 * tokens * total * out_cols,
            bytes_accessed=2 * (3 * rows * total + total * out_cols + rows * members * out_cols),
            transcendentals=per_dev * tokens * tokens,
        ),
    )(head_class, kv_count, kv_blocks[0].transpose(1, 2, 0), queries[0], keys[0], values[0], weight)
    return result[None]


def solution(mesh):
    placed = (
        P("pipe", "seq", None),
        P("pipe", "seq", None),
        P("pipe", "seq", None),
        P("pipe", None, "seq"),
        P("pipe", None),
        P("pipe", None, None, None),
        P("pipe", None),
    )
    return jax.shard_map(
        functools.partial(shards, mesh.shape["pipe"]),
        mesh=mesh, in_specs=placed, out_specs=P("pipe", "seq", None), check_vma=False,
    )
```

```python
import functools

import jax
import jax.numpy as jnp
from jax import lax
from jax.experimental import pallas as pl
from jax.experimental.pallas import tpu as pltpu
from jax.sharding import PartitionSpec as P

FRAMES = 4
BLOCK = 64
MASKED = 131072.0
LOG2E = 1.4426950408889634
TILE = 256
AHEAD = 3
MESH = pl.DeviceIdType.MESH


def kernel(
    members, per_dev, stages,
    classes, counts, lists, queries, keys, values, weight,
    out,
    staged, packed, heads_in, ebuf, bbuf, abuf, wboth, cown, csend, crecv, osend, obuf,
    staging, qkv_send, qkv_recv, qkv_local, w_sems, w_local, up_send, down_send, side_send, a_recv,
    c_send, c_recv, o_send, o_recv,
):
    stage = lax.axis_index("pipe")
    me = lax.axis_index("seq")
    half = lax.rem(me, 2)
    col = me // 2
    side = lax.rem(col, 2)
    level = col // 2
    levels = members // 4
    cols = members // 2
    partner = me + 1 - 2 * half
    across = me + 2 - 4 * side
    following = lax.rem(stage + 1, stages)
    preceding = lax.rem(stage + stages - 1, stages)
    rows, width = queries.shape[0], ebuf.shape[-1]
    tokens = rows * members
    depth = per_dev * width
    out_cols = weight.shape[0]
    tile = TILE
    chunks = tokens // tile
    group = tile // rows
    tensors = (queries, keys, values)
    loads = [
        pltpu.make_async_copy(source, staged.at[which], staging.at[which])
        for which, source in enumerate(tensors)
    ]
    for load in loads:
        load.start()

    def block_at(chunk, place):
        return place * chunks + lax.rem(chunk + place, chunks)

    barrier = pltpu.get_barrier_semaphore()

    def greet(r, carry):
        pl.semaphore_signal(
            barrier, inc=1, device_id={"seq": lax.rem(me + r, members)}, device_id_type=MESH
        )
        return carry

    def greet_preceding(r, carry):
        pl.semaphore_signal(barrier, inc=1, device_id=(preceding, r), device_id_type=MESH)
        return carry

    lax.fori_loop(1, members, greet, 0)
    lax.fori_loop(0, members, greet_preceding, 0)

    my_place = me // chunks
    my_chunk = lax.rem(lax.rem(me, chunks) + chunks * group - my_place, chunks)
    my_position = my_chunk * group + my_place
    for which, load in enumerate(loads):
        load.wait()
        for head in range(per_dev * members):
            packed[head, which] = staged[which, :, head * width : (head + 1) * width]
    own_copies = []
    for slot in range(per_dev):
        copy = pltpu.make_async_copy(
            packed.at[me * per_dev + slot], heads_in.at[slot, my_position], qkv_local.at[slot]
        )
        copy.start()
        own_copies.append(copy)
    pl.semaphore_wait(barrier, 2 * members - 1)

    for slot in range(per_dev):

        def send(r, carry):
            peer = lax.rem(me + r * (members // 2 - 1), members)
            pltpu.make_async_remote_copy(
                src_ref=packed.at[peer * per_dev + slot],
                dst_ref=heads_in.at[slot, my_position],
                send_sem=qkv_send.at[slot],
                recv_sem=qkv_recv.at[slot],
                device_id={"seq": peer},
                device_id_type=MESH,
            ).start()
            return carry

        lax.fori_loop(1, members, send, 0)

    def weight_columns(column, which_half):
        return pl.ds(pl.multiple_of((2 * column + which_half) * depth, depth), depth)

    def own_weight(column, carry):
        pltpu.make_async_copy(
            weight.at[:, weight_columns(column, half)],
            wboth.at[pl.ds(0, out_cols), pl.ds(pl.multiple_of(column * depth, depth), depth)],
            w_local,
        ).start()
        return carry

    lax.fori_loop(0, cols, own_weight, 0)

    nblock = lists.shape[0]
    place = lax.broadcasted_iota(jnp.int32, (tokens, width), 0)
    lane = lax.broadcasted_iota(jnp.int32, (tokens, width), 1)
    token = block_at(place // tile, lax.rem(place, tile) // rows) * rows + lax.rem(place, rows)
    spatial = token // BLOCK
    temporal = lax.rem(token, tokens // FRAMES) // (BLOCK // FRAMES)
    every = lists[...].astype(jnp.float32)
    head_lane = lax.broadcasted_iota(jnp.int32, every.shape, 2)
    entry = lax.broadcasted_iota(jnp.int32, every.shape[:2] + (width,), 1)
    listed_lane = lax.broadcasted_iota(jnp.int32, entry.shape, 2).astype(jnp.float32)
    for slot in range(per_dev):
        head = me * per_dev + slot
        block_of = jnp.where(classes[0, head] == 1, temporal, spatial)
        member = jnp.where(block_of == lane, 1.0, 0.0).astype(jnp.bfloat16)
        ebuf[slot] = member
        entries = jnp.sum(jnp.where(head_lane == head, every, 0.0), axis=2, keepdims=True)
        usable = jnp.where(entry < counts[0, head], 0.0, -MASKED)
        offset = jnp.max(jnp.where(entries == listed_lane, usable, -MASKED), axis=1)
        offset = jnp.concatenate(
            [offset, jnp.zeros((width - nblock, width), jnp.float32)], axis=0
        ).astype(jnp.bfloat16)
        bbuf[slot] = lax.dot_general(
            member, offset, (((1,), (1,)), ((), ())), preferred_element_type=jnp.float32
        ).astype(jnp.bfloat16)
    for copy in own_copies:
        copy.wait()

    scale = LOG2E * width ** (-0.5)
    others = pl.ds(0, members - 1)

    def chunk_rows(chunk):
        return pl.ds(pl.multiple_of(chunk * tile, tile), tile)

    def piece_copy(source_level, slot, chunk, target, sems):
        column = 2 * source_level + side
        piece = abuf.at[column, slot, chunk_rows(chunk)]
        return pltpu.make_async_remote_copy(
            src_ref=piece,
            dst_ref=piece,
            send_sem=sems.at[slot, chunk, source_level],
            recv_sem=a_recv.at[column, slot, chunk],
            device_id={"seq": target},
            device_id_type=MESH,
        )

    def received(column, slot, chunk):
        piece = abuf.at[column, slot, chunk_rows(chunk)]
        pltpu.make_async_copy(piece, piece, a_recv.at[column, slot, chunk]).wait()

    def send_up(source_level, slot, chunk):
        @pl.when(level + 1 < levels)
        def _():
            piece_copy(source_level, slot, chunk, me + 4, up_send).start()

    def send_down(source_level, slot, chunk):
        @pl.when(level >= 1)
        def _():
            piece_copy(source_level, slot, chunk, me - 4, down_send).start()

    def send_side(source_level, slot, chunk):
        piece_copy(source_level, slot, chunk, across, side_send).start()

    def attend(slot, then):
        span = heads_in.at[slot, others]
        pltpu.make_async_copy(span, span, qkv_recv.at[slot]).wait()

        def step(chunk, carry):
            here = chunk_rows(chunk)
            query = heads_in[slot, pl.ds(chunk * group, group), 0].reshape(tile, width)
            key = heads_in[slot, :, 1].reshape(tokens, width)
            value = heads_in[slot, :, 2].reshape(tokens, width)
            wide_query = jnp.concatenate([query, ebuf[slot, here]], axis=1)
            wide_key = jnp.concatenate([key, bbuf[slot]], axis=1)
            scores = lax.dot_general(
                wide_query, wide_key, (((1,), (1,)), ((), ())), preferred_element_type=jnp.float32
            )
            top = jnp.max(scores, axis=1, keepdims=True)
            probs = jnp.exp2((scores - top) * scale).astype(jnp.bfloat16)
            wide_value = jnp.concatenate(
                [value, jnp.ones((tokens, width), jnp.bfloat16)], axis=1
            )
            sums = jnp.dot(probs, wide_value, preferred_element_type=jnp.float32)
            abuf[col, slot, here] = (sums[:, :width] / sums[:, width:]).astype(jnp.bfloat16)
            send_up(level, slot, chunk)
            send_down(level, slot, chunk)
            send_side(level, slot, chunk)
            then(chunk)
            return carry

        lax.fori_loop(0, chunks, step, 0)

    def relay(slot, chunk, first, last):
        def hop(t, carry):
            below = level - 1 - t
            above = level + 1 + t

            @pl.when(below >= 0)
            def _():
                received(2 * below + side, slot, chunk)
                send_up(below, slot, chunk)
                send_side(below, slot, chunk)

            @pl.when(above < levels)
            def _():
                received(2 * above + side, slot, chunk)
                send_down(above, slot, chunk)
                send_side(above, slot, chunk)

            return carry

        lax.fori_loop(first, last, hop, 0)

    def relay_all(slot, first, last):
        def step(chunk, carry):
            relay(slot, chunk, first, last)
            return carry

        lax.fori_loop(0, chunks, step, 0)

    def swap_weight(column):
        @pl.when(column < cols)
        def _():
            pltpu.make_async_remote_copy(
                src_ref=weight.at[:, weight_columns(column, 1 - half)],
                dst_ref=wboth.at[
                    pl.ds(out_cols, out_cols),
                    pl.ds(pl.multiple_of(column * depth, depth), depth),
                ],
                send_sem=w_sems.at[0],
                recv_sem=w_sems.at[1],
                device_id={"seq": partner},
                device_id_type=MESH,
            ).start()

    weight_span = wboth.at[pl.ds(out_cols, out_cols)]
    for slot in range(per_dev):
        before = swap_weight
        if slot > 0:
            before = functools.partial(relay, slot - 1, first=1, last=2)
        attend(slot, before)
        if slot > 0:
            relay_all(slot - 1, 2, levels - 1)
        if slot < per_dev - 1:

            def first_hop(chunk, carry):
                relay(slot, chunk, 0, 1)
                if slot == 0:
                    swap_weight(chunks + chunk)
                return carry

            lax.fori_loop(0, chunks, first_hop, 0)

    def relay_last(chunk, carry):
        relay(per_dev - 1, chunk, 0, levels - 1)
        return carry

    lax.fori_loop(0, AHEAD, relay_last, 0)
    weight_own = wboth.at[pl.ds(0, out_cols)]
    pltpu.make_async_copy(weight_own, weight_own, w_local).wait()
    pltpu.make_async_copy(weight_span, weight_span, w_sems.at[1]).wait()

    def chunk_copy(chunk):
        here = chunk_rows(chunk)
        return pltpu.make_async_remote_copy(
            src_ref=csend.at[here],
            dst_ref=crecv.at[here],
            send_sem=c_send.at[chunk],
            recv_sem=c_recv.at[chunk],
            device_id={"seq": partner},
            device_id_type=MESH,
        )

    def row_copy(chunk, q):
        start = pl.multiple_of((chunk * group + q) * rows, rows)
        return pltpu.make_async_remote_copy(
            src_ref=osend.at[pl.ds(start, rows)],
            dst_ref=obuf.at[me],
            send_sem=o_send.at[chunk * group + q],
            recv_sem=o_recv.at[me],
            device_id=(following, block_at(chunk, q)),
            device_id_type=MESH,
        )

    def hand(chunk):
        here = chunk_rows(chunk)
        chunk_copy(chunk).wait_recv()
        osend[here] = (cown[here] + crecv[here].astype(jnp.float32)).astype(jnp.bfloat16)
        for q in range(group):
            row_copy(chunk, lax.rem(level + q, group)).start()

    def finish(chunk, carry):
        here = chunk_rows(chunk)

        @pl.when(chunk + AHEAD < chunks)
        def _():
            relay_last(chunk + AHEAD, 0)

        def from_side(source_level, inner):
            for slot in range(per_dev):
                received(2 * source_level + 1 - side, slot, chunk)
            return inner

        lax.fori_loop(0, levels, from_side, 0)
        piece = jnp.concatenate(
            [abuf[column, slot, here] for column in range(cols) for slot in range(per_dev)], axis=1
        )
        shares = lax.dot_general(
            piece, wboth[...], (((1,), (1,)), ((), ())), preferred_element_type=jnp.float32
        )
        csend[here] = shares[:, out_cols:].astype(jnp.bfloat16)
        chunk_copy(chunk).start()
        cown[here] = shares[:, :out_cols]

        @pl.when(chunk >= 1)
        def _():
            hand(chunk - 1)

        return carry

    lax.fori_loop(0, chunks, finish, 0)
    hand(chunks - 1)

    for slot in range(per_dev):
        span = heads_in.at[slot, others]
        pltpu.make_async_copy(span, span, qkv_send.at[slot]).wait()
    pltpu.make_async_copy(weight_span, weight_span, w_sems.at[0]).wait()

    def left(chunk, carry):
        for slot in range(per_dev):

            def from_level(source_level, inner):
                @pl.when((level + 1 < levels) & (source_level <= level))
                def _():
                    piece_copy(source_level, slot, chunk, across, up_send).wait_send()

                @pl.when((level >= 1) & (source_level >= level))
                def _():
                    piece_copy(source_level, slot, chunk, across, down_send).wait_send()

                piece_copy(source_level, slot, chunk, across, side_send).wait_send()
                return inner

            lax.fori_loop(0, levels, from_level, 0)
        chunk_copy(chunk).wait_send()
        for q in range(group):
            row_copy(chunk, q).wait_send()
        return carry

    lax.fori_loop(0, chunks, left, 0)

    def arrived(source, carry):
        pltpu.make_async_copy(obuf.at[source], obuf.at[source], o_recv.at[source]).wait()
        return carry

    lax.fori_loop(0, members, arrived, 0)
    pair = 2 * out_cols
    for i in range(members // 2):
        out[:, i * pair : (i + 1) * pair] = jnp.concatenate([obuf[2 * i], obuf[2 * i + 1]], axis=1)


def shards(stages, queries, keys, values, out_weight, head_class, kv_blocks, kv_count):
    members = lax.axis_size("seq")
    heads = head_class.shape[1]
    per_dev = heads // members
    rows, total = queries.shape[1:]
    width = total // heads
    tokens = rows * members
    out_cols = out_weight.shape[2]
    cols = members // 2
    depth = per_dev * width
    weight = out_weight[0].T
    bf16, f32 = jnp.bfloat16, jnp.float32
    dma = pltpu.SemaphoreType.DMA
    vmem = pl.BlockSpec(memory_space=pltpu.VMEM)
    smem = pl.BlockSpec(memory_space=pltpu.SMEM)
    hbm = pl.BlockSpec(memory_space=pl.ANY)
    head_buffer = pltpu.VMEM((per_dev, tokens, width), bf16)
    levels = members // 4
    chunks = tokens // TILE
    result = pl.pallas_call(
        functools.partial(kernel, members, per_dev, stages),
        out_shape=jax.ShapeDtypeStruct((rows, members * out_cols), bf16),
        in_specs=[smem, smem, vmem, hbm, hbm, hbm, hbm],
        out_specs=vmem,
        scratch_shapes=[
            pltpu.VMEM((3, rows, total), bf16),
            pltpu.VMEM((heads, 3, rows, width), bf16),
            pltpu.VMEM((per_dev, members, 3, rows, width), bf16),
            head_buffer, head_buffer,
            pltpu.VMEM((cols, per_dev, tokens, width), bf16),
            pltpu.VMEM((2 * out_cols, cols * depth), bf16),
            pltpu.VMEM((tokens, out_cols), f32),
            pltpu.VMEM((tokens, out_cols), bf16),
            pltpu.VMEM((tokens, out_cols), bf16),
            pltpu.VMEM((tokens, out_cols), bf16),
            pltpu.VMEM((members, rows, out_cols), bf16),
            dma((3,)), dma((per_dev,)), dma((per_dev,)), dma((per_dev,)),
            dma((2,)), dma,
            dma((per_dev, chunks, levels)), dma((per_dev, chunks, levels)),
            dma((per_dev, chunks, levels)), dma((cols, per_dev, chunks)),
            dma((chunks,)), dma((chunks,)),
            dma((members,)), dma((members,)),
        ],
        compiler_params=pltpu.CompilerParams(
            collective_id=0, has_side_effects=True, vmem_limit_bytes=60 * 1024 * 1024
        ),
        cost_estimate=pl.CostEstimate(
            flops=4 * tokens * tokens * depth + 2 * tokens * total * out_cols,
            bytes_accessed=2 * (3 * rows * total + total * out_cols + rows * members * out_cols),
            transcendentals=per_dev * tokens * tokens,
        ),
    )(head_class, kv_count, kv_blocks[0].transpose(1, 2, 0), queries[0], keys[0], values[0], weight)
    return result[None]


def solution(mesh):
    placed = (
        P("pipe", "seq", None),
        P("pipe", "seq", None),
        P("pipe", "seq", None),
        P("pipe", None, "seq"),
        P("pipe", None),
        P("pipe", None, None, None),
        P("pipe", None),
    )
    return jax.shard_map(
        functools.partial(shards, mesh.shape["pipe"]),
        mesh=mesh, in_specs=placed, out_specs=P("pipe", "seq", None), check_vma=False,
    )
```

```python
import functools

import jax
import jax.numpy as jnp
from jax import lax
from jax.experimental import pallas as pl
from jax.experimental.pallas import tpu as pltpu
from jax.sharding import PartitionSpec as P

FRAMES = 4
BLOCK = 64
MASKED = 131072.0
LOG2E = 1.4426950408889634
TILE = 256
AHEAD = 3
MESH = pl.DeviceIdType.MESH


def kernel(
    members, per_dev, stages,
    classes, counts, lists, queries, keys, values, weight,
    out,
    staged, packed, heads_in, ebuf, bbuf, abuf, wboth, cown, csend, crecv, osend, obuf,
    staging, qkv_send, qkv_recv, qkv_local, w_sems, w_local, up_send, down_send, side_send, a_recv,
    c_send, c_recv, o_send, o_recv,
):
    stage = lax.axis_index("pipe")
    me = lax.axis_index("seq")
    odd = lax.rem(stage, 2)
    half_step, side_step = 1 + odd, 2 - odd
    bits = (lax.rem(me, 2), lax.rem(me // 2, 2))
    half = bits[0] + odd * (bits[1] - bits[0])
    side = bits[1] + odd * (bits[0] - bits[1])
    level = me // 4
    levels = members // 4
    cols = members // 2
    col = 2 * level + side
    partner = me + half_step * (1 - 2 * half)
    across = me + side_step * (1 - 2 * side)
    following = lax.rem(stage + 1, stages)
    preceding = lax.rem(stage + stages - 1, stages)
    rows, width = queries.shape[0], ebuf.shape[-1]
    tokens = rows * members
    depth = per_dev * width
    out_cols = weight.shape[0]
    tile = TILE
    chunks = tokens // tile
    group = tile // rows
    tensors = (queries, keys, values)
    loads = [
        pltpu.make_async_copy(source, staged.at[which], staging.at[which])
        for which, source in enumerate(tensors)
    ]
    for load in loads:
        load.start()

    def block_at(chunk, place):
        return place * chunks + lax.rem(chunk + place, chunks)

    barrier = pltpu.get_barrier_semaphore()

    def greet(r, carry):
        pl.semaphore_signal(
            barrier, inc=1, device_id={"seq": lax.rem(me + r, members)}, device_id_type=MESH
        )
        return carry

    def greet_preceding(r, carry):
        pl.semaphore_signal(barrier, inc=1, device_id=(preceding, r), device_id_type=MESH)
        return carry

    lax.fori_loop(1, members, greet, 0)
    lax.fori_loop(0, members, greet_preceding, 0)

    my_place = me // chunks
    my_chunk = lax.rem(lax.rem(me, chunks) + chunks * group - my_place, chunks)
    my_position = my_chunk * group + my_place
    for which, load in enumerate(loads):
        load.wait()
        for head in range(per_dev * members):
            packed[head, which] = staged[which, :, head * width : (head + 1) * width]
    own_copies = []
    for slot in range(per_dev):
        copy = pltpu.make_async_copy(
            packed.at[me * per_dev + slot], heads_in.at[slot, my_position], qkv_local.at[slot]
        )
        copy.start()
        own_copies.append(copy)
    pl.semaphore_wait(barrier, 2 * members - 1)

    def weight_columns(column, which_half):
        owner = (column // 2) * 4 + lax.rem(column, 2) * side_step + which_half * half_step
        return pl.ds(pl.multiple_of(owner * depth, depth), depth)

    def swap_weight(column, carry):
        pltpu.make_async_remote_copy(
            src_ref=weight.at[:, weight_columns(column, 1 - half)],
            dst_ref=wboth.at[
                pl.ds(out_cols, out_cols),
                pl.ds(pl.multiple_of(column * depth, depth), depth),
            ],
            send_sem=w_sems.at[0],
            recv_sem=w_sems.at[1],
            device_id={"seq": partner},
            device_id_type=MESH,
        ).start()
        return carry

    for slot in range(per_dev):

        def send(r, carry):
            peer = lax.rem(me + r * (members // 2 - 1), members)
            pltpu.make_async_remote_copy(
                src_ref=packed.at[peer * per_dev + slot],
                dst_ref=heads_in.at[slot, my_position],
                send_sem=qkv_send.at[slot],
                recv_sem=qkv_recv.at[slot],
                device_id={"seq": peer},
                device_id_type=MESH,
            ).start()
            return carry

        lax.fori_loop(1, members, send, 0)
        if slot == 0:
            lax.fori_loop(0, cols, swap_weight, 0)

    def own_weight(column, carry):
        pltpu.make_async_copy(
            weight.at[:, weight_columns(column, half)],
            wboth.at[pl.ds(0, out_cols), pl.ds(pl.multiple_of(column * depth, depth), depth)],
            w_local,
        ).start()
        return carry

    lax.fori_loop(0, cols, own_weight, 0)

    nblock = lists.shape[0]
    place = lax.broadcasted_iota(jnp.int32, (tokens, width), 0)
    lane = lax.broadcasted_iota(jnp.int32, (tokens, width), 1)
    token = block_at(place // tile, lax.rem(place, tile) // rows) * rows + lax.rem(place, rows)
    spatial = token // BLOCK
    temporal = lax.rem(token, tokens // FRAMES) // (BLOCK // FRAMES)
    every = lists[...].astype(jnp.float32)
    head_lane = lax.broadcasted_iota(jnp.int32, every.shape, 2)
    entry = lax.broadcasted_iota(jnp.int32, every.shape[:2] + (width,), 1)
    listed_lane = lax.broadcasted_iota(jnp.int32, entry.shape, 2).astype(jnp.float32)
    for slot in range(per_dev):
        head = me * per_dev + slot
        block_of = jnp.where(classes[0, head] == 1, temporal, spatial)
        member = jnp.where(block_of == lane, 1.0, 0.0).astype(jnp.bfloat16)
        ebuf[slot] = member
        entries = jnp.sum(jnp.where(head_lane == head, every, 0.0), axis=2, keepdims=True)
        usable = jnp.where(entry < counts[0, head], 0.0, -MASKED)
        offset = jnp.max(jnp.where(entries == listed_lane, usable, -MASKED), axis=1)
        offset = jnp.concatenate(
            [offset, jnp.zeros((width - nblock, width), jnp.float32)], axis=0
        ).astype(jnp.bfloat16)
        bbuf[slot] = lax.dot_general(
            member, offset, (((1,), (1,)), ((), ())), preferred_element_type=jnp.float32
        ).astype(jnp.bfloat16)
    for copy in own_copies:
        copy.wait()

    scale = LOG2E * width ** (-0.5)
    others = pl.ds(0, members - 1)

    def chunk_rows(chunk):
        return pl.ds(pl.multiple_of(chunk * tile, tile), tile)

    def piece_copy(source_level, slot, chunk, target, sems):
        column = 2 * source_level + side
        piece = abuf.at[column, slot, chunk_rows(chunk)]
        return pltpu.make_async_remote_copy(
            src_ref=piece,
            dst_ref=piece,
            send_sem=sems.at[slot, chunk, source_level],
            recv_sem=a_recv.at[column, slot, chunk],
            device_id={"seq": target},
            device_id_type=MESH,
        )

    def received(column, slot, chunk):
        piece = abuf.at[column, slot, chunk_rows(chunk)]
        pltpu.make_async_copy(piece, piece, a_recv.at[column, slot, chunk]).wait()

    def send_up(source_level, slot, chunk):
        @pl.when(level + 1 < levels)
        def _():
            piece_copy(source_level, slot, chunk, me + 4, up_send).start()

    def send_down(source_level, slot, chunk):
        @pl.when(level >= 1)
        def _():
            piece_copy(source_level, slot, chunk, me - 4, down_send).start()

    def send_side(source_level, slot, chunk):
        piece_copy(source_level, slot, chunk, across, side_send).start()

    def attend(slot, then):
        span = heads_in.at[slot, others]
        pltpu.make_async_copy(span, span, qkv_recv.at[slot]).wait()

        def step(chunk, carry):
            here = chunk_rows(chunk)
            query = heads_in[slot, pl.ds(chunk * group, group), 0].reshape(tile, width)
            key = heads_in[slot, :, 1].reshape(tokens, width)
            value = heads_in[slot, :, 2].reshape(tokens, width)
            wide_query = jnp.concatenate([query, ebuf[slot, here]], axis=1)
            wide_key = jnp.concatenate([key, bbuf[slot]], axis=1)
            scores = lax.dot_general(
                wide_query, wide_key, (((1,), (1,)), ((), ())), preferred_element_type=jnp.float32
            )
            top = jnp.max(scores, axis=1, keepdims=True)
            probs = jnp.exp2((scores - top) * scale).astype(jnp.bfloat16)
            wide_value = jnp.concatenate(
                [value, jnp.ones((tokens, width), jnp.bfloat16)], axis=1
            )
            sums = jnp.dot(probs, wide_value, preferred_element_type=jnp.float32)
            abuf[col, slot, here] = (sums[:, :width] / sums[:, width:]).astype(jnp.bfloat16)
            send_up(level, slot, chunk)
            send_down(level, slot, chunk)
            send_side(level, slot, chunk)
            if then is not None:
                then(chunk)
            return carry

        lax.fori_loop(0, chunks, step, 0)

    def relay(slot, chunk, first, last):
        def hop(t, carry):
            below = level - 1 - t
            above = level + 1 + t

            @pl.when(below >= 0)
            def _():
                received(2 * below + side, slot, chunk)
                send_up(below, slot, chunk)
                send_side(below, slot, chunk)

            @pl.when(above < levels)
            def _():
                received(2 * above + side, slot, chunk)
                send_down(above, slot, chunk)
                send_side(above, slot, chunk)

            return carry

        lax.fori_loop(first, last, hop, 0)

    def relay_all(slot, first, last):
        def step(chunk, carry):
            relay(slot, chunk, first, last)
            return carry

        lax.fori_loop(0, chunks, step, 0)

    weight_span = wboth.at[pl.ds(out_cols, out_cols)]
    for slot in range(per_dev):
        before = None
        if slot > 0:
            before = functools.partial(relay, slot - 1, first=1, last=2)
        attend(slot, before)
        if slot > 0:
            relay_all(slot - 1, 2, levels - 1)
        if slot < per_dev - 1:
            relay_all(slot, 0, 1)

    def relay_last(chunk, carry):
        relay(per_dev - 1, chunk, 0, levels - 1)
        return carry

    lax.fori_loop(0, AHEAD, relay_last, 0)
    weight_own = wboth.at[pl.ds(0, out_cols)]
    pltpu.make_async_copy(weight_own, weight_own, w_local).wait()
    pltpu.make_async_copy(weight_span, weight_span, w_sems.at[1]).wait()

    def chunk_copy(chunk):
        here = chunk_rows(chunk)
        return pltpu.make_async_remote_copy(
            src_ref=csend.at[here],
            dst_ref=crecv.at[here],
            send_sem=c_send.at[chunk],
            recv_sem=c_recv.at[chunk],
            device_id={"seq": partner},
            device_id_type=MESH,
        )

    def row_copy(chunk, q):
        start = pl.multiple_of((chunk * group + q) * rows, rows)
        return pltpu.make_async_remote_copy(
            src_ref=osend.at[pl.ds(start, rows)],
            dst_ref=obuf.at[me],
            send_sem=o_send.at[chunk * group + q],
            recv_sem=o_recv.at[me],
            device_id=(following, block_at(chunk, q)),
            device_id_type=MESH,
        )

    def hand(chunk):
        here = chunk_rows(chunk)
        chunk_copy(chunk).wait_recv()
        osend[here] = (cown[here] + crecv[here].astype(jnp.float32)).astype(jnp.bfloat16)
        for q in range(group):
            row_copy(chunk, lax.rem(level + q, group)).start()

    def finish(chunk, carry):
        here = chunk_rows(chunk)

        @pl.when(chunk + AHEAD < chunks)
        def _():
            relay_last(chunk + AHEAD, 0)

        def from_side(source_level, inner):
            for slot in range(per_dev):
                received(2 * source_level + 1 - side, slot, chunk)
            return inner

        lax.fori_loop(0, levels, from_side, 0)
        piece = jnp.concatenate(
            [abuf[column, slot, here] for column in range(cols) for slot in range(per_dev)], axis=1
        )
        shares = lax.dot_general(
            piece, wboth[...], (((1,), (1,)), ((), ())), preferred_element_type=jnp.float32
        )
        csend[here] = shares[:, out_cols:].astype(jnp.bfloat16)
        chunk_copy(chunk).start()
        cown[here] = shares[:, :out_cols]

        @pl.when(chunk >= 1)
        def _():
            hand(chunk - 1)

        return carry

    lax.fori_loop(0, chunks, finish, 0)
    hand(chunks - 1)

    for slot in range(per_dev):
        span = heads_in.at[slot, others]
        pltpu.make_async_copy(span, span, qkv_send.at[slot]).wait()
    pltpu.make_async_copy(weight_span, weight_span, w_sems.at[0]).wait()

    def left(chunk, carry):
        for slot in range(per_dev):

            def from_level(source_level, inner):
                @pl.when((level + 1 < levels) & (source_level <= level))
                def _():
                    piece_copy(source_level, slot, chunk, across, up_send).wait_send()

                @pl.when((level >= 1) & (source_level >= level))
                def _():
                    piece_copy(source_level, slot, chunk, across, down_send).wait_send()

                piece_copy(source_level, slot, chunk, across, side_send).wait_send()
                return inner

            lax.fori_loop(0, levels, from_level, 0)
        chunk_copy(chunk).wait_send()
        for q in range(group):
            row_copy(chunk, q).wait_send()
        return carry

    lax.fori_loop(0, chunks, left, 0)

    def arrived(source, carry):
        pltpu.make_async_copy(obuf.at[source], obuf.at[source], o_recv.at[source]).wait()
        return carry

    lax.fori_loop(0, members, arrived, 0)
    pair = 2 * out_cols
    for i in range(members // 2):
        out[:, i * pair : (i + 1) * pair] = jnp.concatenate([obuf[2 * i], obuf[2 * i + 1]], axis=1)


def shards(stages, queries, keys, values, out_weight, head_class, kv_blocks, kv_count):
    members = lax.axis_size("seq")
    heads = head_class.shape[1]
    per_dev = heads // members
    rows, total = queries.shape[1:]
    width = total // heads
    tokens = rows * members
    out_cols = out_weight.shape[2]
    cols = members // 2
    depth = per_dev * width
    weight = out_weight[0].T
    bf16, f32 = jnp.bfloat16, jnp.float32
    dma = pltpu.SemaphoreType.DMA
    vmem = pl.BlockSpec(memory_space=pltpu.VMEM)
    smem = pl.BlockSpec(memory_space=pltpu.SMEM)
    hbm = pl.BlockSpec(memory_space=pl.ANY)
    head_buffer = pltpu.VMEM((per_dev, tokens, width), bf16)
    levels = members // 4
    chunks = tokens // TILE
    result = pl.pallas_call(
        functools.partial(kernel, members, per_dev, stages),
        out_shape=jax.ShapeDtypeStruct((rows, members * out_cols), bf16),
        in_specs=[smem, smem, vmem, hbm, hbm, hbm, hbm],
        out_specs=vmem,
        scratch_shapes=[
            pltpu.VMEM((3, rows, total), bf16),
            pltpu.VMEM((heads, 3, rows, width), bf16),
            pltpu.VMEM((per_dev, members, 3, rows, width), bf16),
            head_buffer, head_buffer,
            pltpu.VMEM((cols, per_dev, tokens, width), bf16),
            pltpu.VMEM((2 * out_cols, cols * depth), bf16),
            pltpu.VMEM((tokens, out_cols), f32),
            pltpu.VMEM((tokens, out_cols), bf16),
            pltpu.VMEM((tokens, out_cols), bf16),
            pltpu.VMEM((tokens, out_cols), bf16),
            pltpu.VMEM((members, rows, out_cols), bf16),
            dma((3,)), dma((per_dev,)), dma((per_dev,)), dma((per_dev,)),
            dma((2,)), dma,
            dma((per_dev, chunks, levels)), dma((per_dev, chunks, levels)),
            dma((per_dev, chunks, levels)), dma((cols, per_dev, chunks)),
            dma((chunks,)), dma((chunks,)),
            dma((members,)), dma((members,)),
        ],
        compiler_params=pltpu.CompilerParams(
            collective_id=0, has_side_effects=True, vmem_limit_bytes=60 * 1024 * 1024
        ),
        cost_estimate=pl.CostEstimate(
            flops=4 * tokens * tokens * depth + 2 * tokens * total * out_cols,
            bytes_accessed=2 * (3 * rows * total + total * out_cols + rows * members * out_cols),
            transcendentals=per_dev * tokens * tokens,
        ),
    )(head_class, kv_count, kv_blocks[0].transpose(1, 2, 0), queries[0], keys[0], values[0], weight)
    return result[None]


def solution(mesh):
    placed = (
        P("pipe", "seq", None),
        P("pipe", "seq", None),
        P("pipe", "seq", None),
        P("pipe", None, "seq"),
        P("pipe", None),
        P("pipe", None, None, None),
        P("pipe", None),
    )
    return jax.shard_map(
        functools.partial(shards, mesh.shape["pipe"]),
        mesh=mesh, in_specs=placed, out_specs=P("pipe", "seq", None), check_vma=False,
    )
```

```python
import functools

import jax
import jax.numpy as jnp
from jax import lax
from jax.experimental import pallas as pl
from jax.experimental.pallas import tpu as pltpu
from jax.sharding import PartitionSpec as P

FRAMES = 4
BLOCK = 64
MASKED = 131072.0
LOG2E = 1.4426950408889634
TILE = 256
MESH = pl.DeviceIdType.MESH


def kernel(
    members, per_dev, stages,
    classes, counts, lists, queries, keys, values, weight,
    out,
    staged, packed, heads_in, ebuf, bbuf, abuf, wboth, cacc, cown, csend, crecv, osend, obuf,
    staging, qkv_send, qkv_recv, qkv_local, w_sems, w_local, up_send, down_send, side_send, a_recv,
    c_send, c_recv, o_send, o_recv,
):
    stage = lax.axis_index("pipe")
    me = lax.axis_index("seq")
    odd = lax.rem(stage, 2)
    half_step, side_step = 1 + odd, 2 - odd
    bits = (lax.rem(me, 2), lax.rem(me // 2, 2))
    half = bits[0] + odd * (bits[1] - bits[0])
    side = bits[1] + odd * (bits[0] - bits[1])
    level = me // 4
    levels = members // 4
    cols = members // 2
    col = 2 * level + side
    partner = me + half_step * (1 - 2 * half)
    across = me + side_step * (1 - 2 * side)
    following = lax.rem(stage + 1, stages)
    preceding = lax.rem(stage + stages - 1, stages)
    rows, width = queries.shape[0], ebuf.shape[-1]
    tokens = rows * members
    depth = per_dev * width
    out_cols = weight.shape[0]
    tile = TILE
    chunks = tokens // tile
    group = tile // rows
    tensors = (queries, keys, values)
    loads = [
        pltpu.make_async_copy(source, staged.at[which], staging.at[which])
        for which, source in enumerate(tensors)
    ]
    for load in loads:
        load.start()

    def block_at(chunk, place):
        return place * chunks + lax.rem(chunk + place, chunks)

    barrier = pltpu.get_barrier_semaphore()

    def greet(r, carry):
        pl.semaphore_signal(
            barrier, inc=1, device_id={"seq": lax.rem(me + r, members)}, device_id_type=MESH
        )
        return carry

    def greet_preceding(r, carry):
        pl.semaphore_signal(barrier, inc=1, device_id=(preceding, r), device_id_type=MESH)
        return carry

    lax.fori_loop(1, members, greet, 0)
    lax.fori_loop(0, members, greet_preceding, 0)

    my_place = me // chunks
    my_chunk = lax.rem(lax.rem(me, chunks) + chunks * group - my_place, chunks)
    my_position = my_chunk * group + my_place
    for which, load in enumerate(loads):
        load.wait()
        for head in range(per_dev * members):
            packed[head, which] = staged[which, :, head * width : (head + 1) * width]
    own_copies = []
    for slot in range(per_dev):
        copy = pltpu.make_async_copy(
            packed.at[me * per_dev + slot], heads_in.at[slot, my_position], qkv_local.at[slot]
        )
        copy.start()
        own_copies.append(copy)
    pl.semaphore_wait(barrier, 2 * members - 1)

    def weight_columns(column, which_half):
        owner = (column // 2) * 4 + lax.rem(column, 2) * side_step + which_half * half_step
        return pl.ds(pl.multiple_of(owner * depth, depth), depth)

    def swap_weight(column, carry):
        pltpu.make_async_remote_copy(
            src_ref=weight.at[:, weight_columns(column, 1 - half)],
            dst_ref=wboth.at[
                pl.ds(out_cols, out_cols),
                pl.ds(pl.multiple_of(column * depth, depth), depth),
            ],
            send_sem=w_sems.at[0],
            recv_sem=w_sems.at[1],
            device_id={"seq": partner},
            device_id_type=MESH,
        ).start()
        return carry

    for slot in range(per_dev):

        def send(r, carry):
            peer = lax.rem(me + r * (members // 2 - 1), members)
            pltpu.make_async_remote_copy(
                src_ref=packed.at[peer * per_dev + slot],
                dst_ref=heads_in.at[slot, my_position],
                send_sem=qkv_send.at[slot],
                recv_sem=qkv_recv.at[slot],
                device_id={"seq": peer},
                device_id_type=MESH,
            ).start()
            return carry

        lax.fori_loop(1, members, send, 0)
        if slot == 0:
            lax.fori_loop(0, cols, swap_weight, 0)

    def own_weight(column, carry):
        pltpu.make_async_copy(
            weight.at[:, weight_columns(column, half)],
            wboth.at[pl.ds(0, out_cols), pl.ds(pl.multiple_of(column * depth, depth), depth)],
            w_local,
        ).start()
        return carry

    lax.fori_loop(0, cols, own_weight, 0)

    nblock = lists.shape[0]
    place = lax.broadcasted_iota(jnp.int32, (tokens, width), 0)
    lane = lax.broadcasted_iota(jnp.int32, (tokens, width), 1)
    token = block_at(place // tile, lax.rem(place, tile) // rows) * rows + lax.rem(place, rows)
    spatial = token // BLOCK
    temporal = lax.rem(token, tokens // FRAMES) // (BLOCK // FRAMES)
    every = lists[...].astype(jnp.float32)
    head_lane = lax.broadcasted_iota(jnp.int32, every.shape, 2)
    entry = lax.broadcasted_iota(jnp.int32, every.shape[:2] + (width,), 1)
    listed_lane = lax.broadcasted_iota(jnp.int32, entry.shape, 2).astype(jnp.float32)
    for slot in range(per_dev):
        head = me * per_dev + slot
        block_of = jnp.where(classes[0, head] == 1, temporal, spatial)
        member = jnp.where(block_of == lane, 1.0, 0.0).astype(jnp.bfloat16)
        ebuf[slot] = member
        entries = jnp.sum(jnp.where(head_lane == head, every, 0.0), axis=2, keepdims=True)
        usable = jnp.where(entry < counts[0, head], 0.0, -MASKED)
        offset = jnp.max(jnp.where(entries == listed_lane, usable, -MASKED), axis=1)
        offset = jnp.concatenate(
            [offset, jnp.zeros((width - nblock, width), jnp.float32)], axis=0
        ).astype(jnp.bfloat16)
        bbuf[slot] = lax.dot_general(
            member, offset, (((1,), (1,)), ((), ())), preferred_element_type=jnp.float32
        ).astype(jnp.bfloat16)
    for copy in own_copies:
        copy.wait()

    scale = LOG2E * width ** (-0.5)
    others = pl.ds(0, members - 1)

    def chunk_rows(chunk):
        return pl.ds(pl.multiple_of(chunk * tile, tile), tile)

    def piece_copy(source_level, slot, chunk, target, sems):
        column = 2 * source_level + side
        piece = abuf.at[column, slot, chunk_rows(chunk)]
        return pltpu.make_async_remote_copy(
            src_ref=piece,
            dst_ref=piece,
            send_sem=sems.at[slot, chunk, source_level],
            recv_sem=a_recv.at[column, slot, chunk],
            device_id={"seq": target},
            device_id_type=MESH,
        )

    def received(column, slot, chunk):
        piece = abuf.at[column, slot, chunk_rows(chunk)]
        pltpu.make_async_copy(piece, piece, a_recv.at[column, slot, chunk]).wait()

    def send_up(source_level, slot, chunk):
        @pl.when(level + 1 < levels)
        def _():
            piece_copy(source_level, slot, chunk, me + 4, up_send).start()

    def send_down(source_level, slot, chunk):
        @pl.when(level >= 1)
        def _():
            piece_copy(source_level, slot, chunk, me - 4, down_send).start()

    def send_side(source_level, slot, chunk):
        piece_copy(source_level, slot, chunk, across, side_send).start()

    def attend(slot, then):
        span = heads_in.at[slot, others]
        pltpu.make_async_copy(span, span, qkv_recv.at[slot]).wait()

        def step(chunk, carry):
            here = chunk_rows(chunk)
            query = heads_in[slot, pl.ds(chunk * group, group), 0].reshape(tile, width)
            key = heads_in[slot, :, 1].reshape(tokens, width)
            value = heads_in[slot, :, 2].reshape(tokens, width)
            wide_query = jnp.concatenate([query, ebuf[slot, here]], axis=1)
            wide_key = jnp.concatenate([key, bbuf[slot]], axis=1)
            scores = lax.dot_general(
                wide_query, wide_key, (((1,), (1,)), ((), ())), preferred_element_type=jnp.float32
            )
            top = jnp.max(scores, axis=1, keepdims=True)
            probs = jnp.exp2((scores - top) * scale).astype(jnp.bfloat16)
            wide_value = jnp.concatenate(
                [value, jnp.ones((tokens, width), jnp.bfloat16)], axis=1
            )
            sums = jnp.dot(probs, wide_value, preferred_element_type=jnp.float32)
            abuf[col, slot, here] = (sums[:, :width] / sums[:, width:]).astype(jnp.bfloat16)
            send_up(level, slot, chunk)
            send_down(level, slot, chunk)
            send_side(level, slot, chunk)
            if then is not None:
                then(chunk)
            return carry

        lax.fori_loop(0, chunks, step, 0)

    def relay(slot, chunk, first, last):
        def hop(t, carry):
            below = level - 1 - t
            above = level + 1 + t

            @pl.when(below >= 0)
            def _():
                received(2 * below + side, slot, chunk)
                send_up(below, slot, chunk)
                send_side(below, slot, chunk)

            @pl.when(above < levels)
            def _():
                received(2 * above + side, slot, chunk)
                send_down(above, slot, chunk)
                send_side(above, slot, chunk)

            return carry

        lax.fori_loop(first, last, hop, 0)

    def relay_all(slot, first, last):
        def step(chunk, carry):
            relay(slot, chunk, first, last)
            return carry

        lax.fori_loop(0, chunks, step, 0)

    weight_span = wboth.at[pl.ds(out_cols, out_cols)]
    for slot in range(per_dev):
        before = None
        if slot > 0:
            before = functools.partial(relay, slot - 1, first=1, last=2)
        attend(slot, before)
        if slot > 0:
            relay_all(slot - 1, 2, levels - 1)
        if slot < per_dev - 1:
            relay_all(slot, 0, 1)

    weight_own = wboth.at[pl.ds(0, out_cols)]
    pltpu.make_async_copy(weight_own, weight_own, w_local).wait()
    pltpu.make_async_copy(weight_span, weight_span, w_sems.at[1]).wait()

    def chunk_copy(chunk):
        here = chunk_rows(chunk)
        return pltpu.make_async_remote_copy(
            src_ref=csend.at[here],
            dst_ref=crecv.at[here],
            send_sem=c_send.at[chunk],
            recv_sem=c_recv.at[chunk],
            device_id={"seq": partner},
            device_id_type=MESH,
        )

    def row_copy(chunk, q):
        start = pl.multiple_of((chunk * group + q) * rows, rows)
        return pltpu.make_async_remote_copy(
            src_ref=osend.at[pl.ds(start, rows)],
            dst_ref=obuf.at[me],
            send_sem=o_send.at[chunk * group + q],
            recv_sem=o_recv.at[me],
            device_id=(following, block_at(chunk, q)),
            device_id_type=MESH,
        )

    def hand(chunk):
        here = chunk_rows(chunk)
        chunk_copy(chunk).wait_recv()
        osend[here] = (cown[here] + crecv[here].astype(jnp.float32)).astype(jnp.bfloat16)
        for q in range(group):
            row_copy(chunk, lax.rem(level + q, group)).start()

    def share(slot, chunk):
        def from_side(source_level, inner):
            received(2 * source_level + 1 - side, slot, chunk)
            return inner

        lax.fori_loop(0, levels, from_side, 0)
        here = chunk_rows(chunk)
        piece = jnp.concatenate([abuf[column, slot, here] for column in range(cols)], axis=1)
        starts = [column * depth + slot * width for column in range(cols)]
        columns = jnp.concatenate([wboth[:, start : start + width] for start in starts], axis=1)
        return lax.dot_general(
            piece, columns, (((1,), (1,)), ((), ())), preferred_element_type=jnp.float32
        )

    def prepare(chunk, carry):
        relay(per_dev - 1, chunk, 0, levels - 1)
        total = share(0, chunk)
        for slot in range(1, per_dev - 1):
            total += share(slot, chunk)
        cacc[chunk_rows(chunk)] = total
        return carry

    def finish(chunk, carry):
        here = chunk_rows(chunk)
        shares = cacc[here] + share(per_dev - 1, chunk)
        csend[here] = shares[:, out_cols:].astype(jnp.bfloat16)
        chunk_copy(chunk).start()
        cown[here] = shares[:, :out_cols]

        @pl.when(chunk >= 1)
        def _():
            hand(chunk - 1)

        return carry

    lax.fori_loop(0, chunks, prepare, 0)
    lax.fori_loop(0, chunks, finish, 0)
    hand(chunks - 1)

    for slot in range(per_dev):
        span = heads_in.at[slot, others]
        pltpu.make_async_copy(span, span, qkv_send.at[slot]).wait()
    pltpu.make_async_copy(weight_span, weight_span, w_sems.at[0]).wait()

    def left(chunk, carry):
        for slot in range(per_dev):

            def from_level(source_level, inner):
                @pl.when((level + 1 < levels) & (source_level <= level))
                def _():
                    piece_copy(source_level, slot, chunk, across, up_send).wait_send()

                @pl.when((level >= 1) & (source_level >= level))
                def _():
                    piece_copy(source_level, slot, chunk, across, down_send).wait_send()

                piece_copy(source_level, slot, chunk, across, side_send).wait_send()
                return inner

            lax.fori_loop(0, levels, from_level, 0)
        chunk_copy(chunk).wait_send()
        for q in range(group):
            row_copy(chunk, q).wait_send()
        return carry

    lax.fori_loop(0, chunks, left, 0)

    def arrived(source, carry):
        pltpu.make_async_copy(obuf.at[source], obuf.at[source], o_recv.at[source]).wait()
        return carry

    lax.fori_loop(0, members, arrived, 0)
    pair = 2 * out_cols
    for i in range(members // 2):
        out[:, i * pair : (i + 1) * pair] = jnp.concatenate([obuf[2 * i], obuf[2 * i + 1]], axis=1)


def shards(stages, queries, keys, values, out_weight, head_class, kv_blocks, kv_count):
    members = lax.axis_size("seq")
    heads = head_class.shape[1]
    per_dev = heads // members
    rows, total = queries.shape[1:]
    width = total // heads
    tokens = rows * members
    out_cols = out_weight.shape[2]
    cols = members // 2
    depth = per_dev * width
    weight = out_weight[0].T
    bf16, f32 = jnp.bfloat16, jnp.float32
    dma = pltpu.SemaphoreType.DMA
    vmem = pl.BlockSpec(memory_space=pltpu.VMEM)
    smem = pl.BlockSpec(memory_space=pltpu.SMEM)
    hbm = pl.BlockSpec(memory_space=pltpu.HBM)
    head_buffer = pltpu.VMEM((per_dev, tokens, width), bf16)
    levels = members // 4
    chunks = tokens // TILE
    result = pl.pallas_call(
        functools.partial(kernel, members, per_dev, stages),
        out_shape=jax.ShapeDtypeStruct((rows, members * out_cols), bf16),
        in_specs=[smem, smem, vmem, hbm, hbm, hbm, hbm],
        out_specs=vmem,
        scratch_shapes=[
            pltpu.VMEM((3, rows, total), bf16),
            pltpu.VMEM((heads, 3, rows, width), bf16),
            pltpu.VMEM((per_dev, members, 3, rows, width), bf16),
            head_buffer, head_buffer,
            pltpu.VMEM((cols, per_dev, tokens, width), bf16),
            pltpu.VMEM((2 * out_cols, cols * depth), bf16),
            pltpu.VMEM((tokens, 2 * out_cols), f32),
            pltpu.VMEM((tokens, out_cols), f32),
            pltpu.VMEM((tokens, out_cols), bf16),
            pltpu.VMEM((tokens, out_cols), bf16),
            pltpu.VMEM((tokens, out_cols), bf16),
            pltpu.VMEM((members, rows, out_cols), bf16),
            dma((3,)), dma((per_dev,)), dma((per_dev,)), dma((per_dev,)),
            dma((2,)), dma,
            dma((per_dev, chunks, levels)), dma((per_dev, chunks, levels)),
            dma((per_dev, chunks, levels)), dma((cols, per_dev, chunks)),
            dma((chunks,)), dma((chunks,)),
            dma((members,)), dma((members,)),
        ],
        compiler_params=pltpu.CompilerParams(
            collective_id=0, has_side_effects=True, vmem_limit_bytes=48 * 1024 * 1024
        ),
        cost_estimate=pl.CostEstimate(
            flops=4 * tokens * tokens * depth + 2 * tokens * total * out_cols,
            bytes_accessed=2 * (3 * rows * total + total * out_cols + rows * members * out_cols),
            transcendentals=per_dev * tokens * tokens,
        ),
    )(head_class, kv_count, kv_blocks[0].transpose(1, 2, 0), queries[0], keys[0], values[0], weight)
    return result[None]


def solution(mesh):
    placed = (
        P("pipe", "seq", None),
        P("pipe", "seq", None),
        P("pipe", "seq", None),
        P("pipe", None, "seq"),
        P("pipe", None),
        P("pipe", None, None, None),
        P("pipe", None),
    )
    return jax.shard_map(
        functools.partial(shards, mesh.shape["pipe"]),
        mesh=mesh, in_specs=placed, out_specs=P("pipe", "seq", None), check_vma=False,
    )
```

```python
import functools

import jax
import jax.numpy as jnp
from jax import lax
from jax.experimental import pallas as pl
from jax.experimental.pallas import tpu as pltpu
from jax.sharding import PartitionSpec as P

FRAMES = 4
BLOCK = 64
MASKED = 131072.0
LOG2E = 1.4426950408889634
TILE = 256
MESH = pl.DeviceIdType.MESH


def kernel(
    members, per_dev, stages,
    classes, counts, lists, queries, keys, values, weight,
    out,
    staged, packed, heads_in, ebuf, bbuf, abuf, wboth, cown, csend, crecv, osend, obuf,
    staging, qkv_send, qkv_recv, qkv_local, w_sems, w_local, up_send, down_send, side_send, a_recv,
    c_send, c_recv, o_send, o_recv,
):
    stage = lax.axis_index("pipe")
    me = lax.axis_index("seq")
    odd = lax.rem(stage, 2)
    half_step, side_step = 1 + odd, 2 - odd
    bits = (lax.rem(me, 2), lax.rem(me // 2, 2))
    half = bits[0] + odd * (bits[1] - bits[0])
    side = bits[1] + odd * (bits[0] - bits[1])
    level = me // 4
    levels = members // 4
    cols = members // 2
    col = 2 * level + side
    partner = me + half_step * (1 - 2 * half)
    across = me + side_step * (1 - 2 * side)
    following = lax.rem(stage + 1, stages)
    preceding = lax.rem(stage + stages - 1, stages)
    rows, width = queries.shape[0], ebuf.shape[-1]
    tokens = rows * members
    depth = per_dev * width
    out_cols = weight.shape[0]
    tile = TILE
    chunks = tokens // tile
    group = tile // rows
    tensors = (queries, keys, values)
    loads = [
        pltpu.make_async_copy(source, staged.at[which], staging.at[which])
        for which, source in enumerate(tensors)
    ]
    for load in loads:
        load.start()

    def block_at(chunk, place):
        return place * chunks + lax.rem(chunk + place, chunks)

    barrier = pltpu.get_barrier_semaphore()

    def greet(r, carry):
        pl.semaphore_signal(
            barrier, inc=1, device_id={"seq": lax.rem(me + r, members)}, device_id_type=MESH
        )
        return carry

    def greet_preceding(r, carry):
        pl.semaphore_signal(barrier, inc=1, device_id=(preceding, r), device_id_type=MESH)
        return carry

    lax.fori_loop(1, members, greet, 0)
    lax.fori_loop(0, members, greet_preceding, 0)

    my_place = me // chunks
    my_chunk = lax.rem(lax.rem(me, chunks) + chunks * group - my_place, chunks)
    my_position = my_chunk * group + my_place
    for which, load in enumerate(loads):
        load.wait()
        for head in range(per_dev * members):
            packed[head, which] = staged[which, :, head * width : (head + 1) * width]
    own_copies = []
    for slot in range(per_dev):
        copy = pltpu.make_async_copy(
            packed.at[me * per_dev + slot], heads_in.at[slot, my_position], qkv_local.at[slot]
        )
        copy.start()
        own_copies.append(copy)
    pl.semaphore_wait(barrier, 2 * members - 1)

    def weight_columns(column, which_half):
        owner = (column // 2) * 4 + lax.rem(column, 2) * side_step + which_half * half_step
        return pl.ds(pl.multiple_of(owner * depth, depth), depth)

    def swap_weight(column, carry):
        pltpu.make_async_remote_copy(
            src_ref=weight.at[:, weight_columns(column, 1 - half)],
            dst_ref=wboth.at[
                pl.ds(out_cols, out_cols),
                pl.ds(pl.multiple_of(column * depth, depth), depth),
            ],
            send_sem=w_sems.at[0],
            recv_sem=w_sems.at[1],
            device_id={"seq": partner},
            device_id_type=MESH,
        ).start()
        return carry

    for slot in range(per_dev):

        def send(r, carry):
            peer = lax.rem(me + r * (members // 2 - 1), members)
            pltpu.make_async_remote_copy(
                src_ref=packed.at[peer * per_dev + slot],
                dst_ref=heads_in.at[slot, my_position],
                send_sem=qkv_send.at[slot],
                recv_sem=qkv_recv.at[slot],
                device_id={"seq": peer},
                device_id_type=MESH,
            ).start()
            return carry

        lax.fori_loop(1, members, send, 0)
        if slot == 0:
            lax.fori_loop(0, cols, swap_weight, 0)

    def own_weight(column, carry):
        pltpu.make_async_copy(
            weight.at[:, weight_columns(column, half)],
            wboth.at[pl.ds(0, out_cols), pl.ds(pl.multiple_of(column * depth, depth), depth)],
            w_local,
        ).start()
        return carry

    lax.fori_loop(0, cols, own_weight, 0)

    nblock = lists.shape[0]
    place = lax.broadcasted_iota(jnp.int32, (tokens, width), 0)
    lane = lax.broadcasted_iota(jnp.int32, (tokens, width), 1)
    token = block_at(place // tile, lax.rem(place, tile) // rows) * rows + lax.rem(place, rows)
    spatial = token // BLOCK
    temporal = lax.rem(token, tokens // FRAMES) // (BLOCK // FRAMES)
    every = lists[...].astype(jnp.float32)
    head_lane = lax.broadcasted_iota(jnp.int32, every.shape, 2)
    entry = lax.broadcasted_iota(jnp.int32, every.shape[:2] + (width,), 1)
    listed_lane = lax.broadcasted_iota(jnp.int32, entry.shape, 2).astype(jnp.float32)
    for slot in range(per_dev):
        head = me * per_dev + slot
        block_of = jnp.where(classes[0, head] == 1, temporal, spatial)
        member = jnp.where(block_of == lane, 1.0, 0.0).astype(jnp.bfloat16)
        ebuf[slot] = member
        entries = jnp.sum(jnp.where(head_lane == head, every, 0.0), axis=2, keepdims=True)
        usable = jnp.where(entry < counts[0, head], 0.0, -MASKED)
        offset = jnp.max(jnp.where(entries == listed_lane, usable, -MASKED), axis=1)
        offset = jnp.concatenate(
            [offset, jnp.zeros((width - nblock, width), jnp.float32)], axis=0
        ).astype(jnp.bfloat16)
        bbuf[slot] = lax.dot_general(
            member, offset, (((1,), (1,)), ((), ())), preferred_element_type=jnp.float32
        ).astype(jnp.bfloat16)
    for copy in own_copies:
        copy.wait()

    scale = LOG2E * width ** (-0.5)
    others = pl.ds(0, members - 1)

    def chunk_rows(chunk):
        return pl.ds(pl.multiple_of(chunk * tile, tile), tile)

    def piece_copy(source_level, slot, chunk, target, sems):
        column = 2 * source_level + side
        piece = abuf.at[column, slot, chunk_rows(chunk)]
        return pltpu.make_async_remote_copy(
            src_ref=piece,
            dst_ref=piece,
            send_sem=sems.at[slot, chunk, source_level],
            recv_sem=a_recv.at[column, slot, chunk],
            device_id={"seq": target},
            device_id_type=MESH,
        )

    def received(column, slot, chunk):
        piece = abuf.at[column, slot, chunk_rows(chunk)]
        pltpu.make_async_copy(piece, piece, a_recv.at[column, slot, chunk]).wait()

    def send_up(source_level, slot, chunk):
        @pl.when(level + 1 < levels)
        def _():
            piece_copy(source_level, slot, chunk, me + 4, up_send).start()

    def send_down(source_level, slot, chunk):
        @pl.when(level >= 1)
        def _():
            piece_copy(source_level, slot, chunk, me - 4, down_send).start()

    def send_side(source_level, slot, chunk):
        piece_copy(source_level, slot, chunk, across, side_send).start()

    def attend(slot, then):
        span = heads_in.at[slot, others]
        pltpu.make_async_copy(span, span, qkv_recv.at[slot]).wait()

        def step(chunk, carry):
            here = chunk_rows(chunk)
            query = heads_in[slot, pl.ds(chunk * group, group), 0].reshape(tile, width)
            key = heads_in[slot, :, 1].reshape(tokens, width)
            value = heads_in[slot, :, 2].reshape(tokens, width)
            wide_query = jnp.concatenate([query, ebuf[slot, here]], axis=1)
            wide_key = jnp.concatenate([key, bbuf[slot]], axis=1)
            scores = lax.dot_general(
                wide_query, wide_key, (((1,), (1,)), ((), ())), preferred_element_type=jnp.float32
            )
            top = jnp.max(scores, axis=1, keepdims=True)
            probs = jnp.exp2((scores - top) * scale).astype(jnp.bfloat16)
            wide_value = jnp.concatenate(
                [value, jnp.ones((tokens, width), jnp.bfloat16)], axis=1
            )
            sums = jnp.dot(probs, wide_value, preferred_element_type=jnp.float32)
            abuf[col, slot, here] = (sums[:, :width] / sums[:, width:]).astype(jnp.bfloat16)
            send_up(level, slot, chunk)
            send_down(level, slot, chunk)
            send_side(level, slot, chunk)
            if then is not None:
                then(chunk)
            return carry

        lax.fori_loop(0, chunks, step, 0)

    def relay(slot, chunk, first, last):
        def hop(t, carry):
            below = level - 1 - t
            above = level + 1 + t

            @pl.when(below >= 0)
            def _():
                received(2 * below + side, slot, chunk)
                send_up(below, slot, chunk)
                send_side(below, slot, chunk)

            @pl.when(above < levels)
            def _():
                received(2 * above + side, slot, chunk)
                send_down(above, slot, chunk)
                send_side(above, slot, chunk)

            return carry

        lax.fori_loop(first, last, hop, 0)

    def wave(n):
        def hop(t, carry):
            piece = n - 1 - t

            @pl.when((piece >= 0) & (piece < per_dev * chunks))
            def _():
                relay(piece // chunks, lax.rem(piece, chunks), t, t + 1)

            return carry

        lax.fori_loop(0, levels - 1, hop, 0)

    weight_span = wboth.at[pl.ds(out_cols, out_cols)]
    for slot in range(per_dev):
        if slot > 0:
            wave(slot * chunks)

        def after(chunk, slot=slot):
            @pl.when(chunk > 0)
            def _():
                wave(slot * chunks + chunk)

        attend(slot, after)

    weight_own = wboth.at[pl.ds(0, out_cols)]
    pltpu.make_async_copy(weight_own, weight_own, w_local).wait()
    pltpu.make_async_copy(weight_span, weight_span, w_sems.at[1]).wait()

    def chunk_copy(chunk):
        here = chunk_rows(chunk)
        return pltpu.make_async_remote_copy(
            src_ref=csend.at[here],
            dst_ref=crecv.at[here],
            send_sem=c_send.at[chunk],
            recv_sem=c_recv.at[chunk],
            device_id={"seq": partner},
            device_id_type=MESH,
        )

    def row_copy(chunk, q):
        start = pl.multiple_of((chunk * group + q) * rows, rows)
        return pltpu.make_async_remote_copy(
            src_ref=osend.at[pl.ds(start, rows)],
            dst_ref=obuf.at[me],
            send_sem=o_send.at[chunk * group + q],
            recv_sem=o_recv.at[me],
            device_id=(following, block_at(chunk, q)),
            device_id_type=MESH,
        )

    def hand(chunk):
        here = chunk_rows(chunk)
        chunk_copy(chunk).wait_recv()
        osend[here] = (cown[here] + crecv[here].astype(jnp.float32)).astype(jnp.bfloat16)
        for q in range(group):
            row_copy(chunk, lax.rem(level + q, group)).start()

    def finish(chunk, carry):
        here = chunk_rows(chunk)

        wave(per_dev * chunks + chunk)

        def from_side(source_level, inner):
            for slot in range(per_dev):
                received(2 * source_level + 1 - side, slot, chunk)
            return inner

        lax.fori_loop(0, levels, from_side, 0)
        piece = jnp.concatenate(
            [abuf[column, slot, here] for column in range(cols) for slot in range(per_dev)], axis=1
        )
        shares = lax.dot_general(
            piece, wboth[...], (((1,), (1,)), ((), ())), preferred_element_type=jnp.float32
        )
        csend[here] = shares[:, out_cols:].astype(jnp.bfloat16)
        chunk_copy(chunk).start()
        cown[here] = shares[:, :out_cols]

        @pl.when(chunk >= 1)
        def _():
            hand(chunk - 1)

        return carry

    lax.fori_loop(0, chunks, finish, 0)
    hand(chunks - 1)

    for slot in range(per_dev):
        span = heads_in.at[slot, others]
        pltpu.make_async_copy(span, span, qkv_send.at[slot]).wait()
    pltpu.make_async_copy(weight_span, weight_span, w_sems.at[0]).wait()

    def left(chunk, carry):
        for slot in range(per_dev):

            def from_level(source_level, inner):
                @pl.when((level + 1 < levels) & (source_level <= level))
                def _():
                    piece_copy(source_level, slot, chunk, across, up_send).wait_send()

                @pl.when((level >= 1) & (source_level >= level))
                def _():
                    piece_copy(source_level, slot, chunk, across, down_send).wait_send()

                piece_copy(source_level, slot, chunk, across, side_send).wait_send()
                return inner

            lax.fori_loop(0, levels, from_level, 0)
        chunk_copy(chunk).wait_send()
        for q in range(group):
            row_copy(chunk, q).wait_send()
        return carry

    lax.fori_loop(0, chunks, left, 0)

    def arrived(source, carry):
        pltpu.make_async_copy(obuf.at[source], obuf.at[source], o_recv.at[source]).wait()
        return carry

    lax.fori_loop(0, members, arrived, 0)
    pair = 2 * out_cols
    for i in range(members // 2):
        out[:, i * pair : (i + 1) * pair] = jnp.concatenate([obuf[2 * i], obuf[2 * i + 1]], axis=1)


def shards(stages, queries, keys, values, out_weight, head_class, kv_blocks, kv_count):
    members = lax.axis_size("seq")
    heads = head_class.shape[1]
    per_dev = heads // members
    rows, total = queries.shape[1:]
    width = total // heads
    tokens = rows * members
    out_cols = out_weight.shape[2]
    cols = members // 2
    depth = per_dev * width
    weight = out_weight[0].T
    bf16, f32 = jnp.bfloat16, jnp.float32
    dma = pltpu.SemaphoreType.DMA
    vmem = pl.BlockSpec(memory_space=pltpu.VMEM)
    smem = pl.BlockSpec(memory_space=pltpu.SMEM)
    hbm = pl.BlockSpec(memory_space=pl.ANY)
    head_buffer = pltpu.VMEM((per_dev, tokens, width), bf16)
    levels = members // 4
    chunks = tokens // TILE
    result = pl.pallas_call(
        functools.partial(kernel, members, per_dev, stages),
        out_shape=jax.ShapeDtypeStruct((rows, members * out_cols), bf16),
        in_specs=[smem, smem, vmem, hbm, hbm, hbm, hbm],
        out_specs=vmem,
        scratch_shapes=[
            pltpu.VMEM((3, rows, total), bf16),
            pltpu.VMEM((heads, 3, rows, width), bf16),
            pltpu.VMEM((per_dev, members, 3, rows, width), bf16),
            head_buffer, head_buffer,
            pltpu.VMEM((cols, per_dev, tokens, width), bf16),
            pltpu.VMEM((2 * out_cols, cols * depth), bf16),
            pltpu.VMEM((tokens, out_cols), f32),
            pltpu.VMEM((tokens, out_cols), bf16),
            pltpu.VMEM((tokens, out_cols), bf16),
            pltpu.VMEM((tokens, out_cols), bf16),
            pltpu.VMEM((members, rows, out_cols), bf16),
            dma((3,)), dma((per_dev,)), dma((per_dev,)), dma((per_dev,)),
            dma((2,)), dma,
            dma((per_dev, chunks, levels)), dma((per_dev, chunks, levels)),
            dma((per_dev, chunks, levels)), dma((cols, per_dev, chunks)),
            dma((chunks,)), dma((chunks,)),
            dma((members,)), dma((members,)),
        ],
        compiler_params=pltpu.CompilerParams(
            collective_id=0, has_side_effects=True, vmem_limit_bytes=60 * 1024 * 1024
        ),
        cost_estimate=pl.CostEstimate(
            flops=4 * tokens * tokens * depth + 2 * tokens * total * out_cols,
            bytes_accessed=2 * (3 * rows * total + total * out_cols + rows * members * out_cols),
            transcendentals=per_dev * tokens * tokens,
        ),
    )(head_class, kv_count, kv_blocks[0].transpose(1, 2, 0), queries[0], keys[0], values[0], weight)
    return result[None]


def solution(mesh):
    placed = (
        P("pipe", "seq", None),
        P("pipe", "seq", None),
        P("pipe", "seq", None),
        P("pipe", None, "seq"),
        P("pipe", None),
        P("pipe", None, None, None),
        P("pipe", None),
    )
    return jax.shard_map(
        functools.partial(shards, mesh.shape["pipe"]),
        mesh=mesh, in_specs=placed, out_specs=P("pipe", "seq", None), check_vma=False,
    )
```

```python
import functools

import jax
import jax.numpy as jnp
from jax import lax
from jax.experimental import pallas as pl
from jax.experimental.pallas import tpu as pltpu
from jax.sharding import PartitionSpec as P

FRAMES = 4
BLOCK = 64
MASKED = 131072.0
LOG2E = 1.4426950408889634
TILE = 256
MESH = pl.DeviceIdType.MESH


def kernel(
    members, per_dev, stages,
    classes, counts, lists, queries, keys, values, weight,
    out,
    staged, packed, heads_in, ebuf, bbuf, abuf, wboth, cown, csend, crecv, osend, obuf,
    staging, qkv_send, qkv_recv, qkv_local, w_sems, w_local, up_send, down_send, side_send, a_recv,
    c_send, c_recv, o_send, o_recv,
):
    stage = lax.axis_index("pipe")
    me = lax.axis_index("seq")
    odd = lax.rem(stage, 2)
    half_step, side_step = 1 + odd, 2 - odd
    bits = (lax.rem(me, 2), lax.rem(me // 2, 2))
    half = bits[0] + odd * (bits[1] - bits[0])
    side = bits[1] + odd * (bits[0] - bits[1])
    level = me // 4
    levels = members // 4
    cols = members // 2
    col = 2 * level + side
    partner = me + half_step * (1 - 2 * half)
    across = me + side_step * (1 - 2 * side)
    following = lax.rem(stage + 1, stages)
    preceding = lax.rem(stage + stages - 1, stages)
    rows, width = queries.shape[0], ebuf.shape[-1]
    tokens = rows * members
    depth = per_dev * width
    out_cols = weight.shape[0]
    tile = TILE
    chunks = tokens // tile
    group = tile // rows
    tensors = (queries, keys, values)
    loads = [
        pltpu.make_async_copy(source, staged.at[which], staging.at[which])
        for which, source in enumerate(tensors)
    ]
    for load in loads:
        load.start()

    def block_at(chunk, place):
        return place * chunks + lax.rem(chunk + place, chunks)

    barrier = pltpu.get_barrier_semaphore()

    def greet(r, carry):
        pl.semaphore_signal(
            barrier, inc=1, device_id={"seq": lax.rem(me + r, members)}, device_id_type=MESH
        )
        return carry

    def greet_preceding(r, carry):
        pl.semaphore_signal(barrier, inc=1, device_id=(preceding, r), device_id_type=MESH)
        return carry

    lax.fori_loop(1, members, greet, 0)
    lax.fori_loop(0, members, greet_preceding, 0)

    my_place = me // chunks
    my_chunk = lax.rem(lax.rem(me, chunks) + chunks * group - my_place, chunks)
    my_position = my_chunk * group + my_place
    for which, load in enumerate(loads):
        load.wait()
        for head in range(per_dev * members):
            packed[head, which] = staged[which, :, head * width : (head + 1) * width]
    own_copies = []
    for slot in range(per_dev):
        copy = pltpu.make_async_copy(
            packed.at[me * per_dev + slot], heads_in.at[slot, my_position], qkv_local.at[slot]
        )
        copy.start()
        own_copies.append(copy)
    pl.semaphore_wait(barrier, 2 * members - 1)

    def weight_columns(column, which_half):
        owner = (column // 2) * 4 + lax.rem(column, 2) * side_step + which_half * half_step
        return pl.ds(pl.multiple_of(owner * depth, depth), depth)

    def swap_weight(column, carry):
        pltpu.make_async_remote_copy(
            src_ref=weight.at[:, weight_columns(column, 1 - half)],
            dst_ref=wboth.at[
                pl.ds(out_cols, out_cols),
                pl.ds(pl.multiple_of(column * depth, depth), depth),
            ],
            send_sem=w_sems.at[0],
            recv_sem=w_sems.at[1],
            device_id={"seq": partner},
            device_id_type=MESH,
        ).start()
        return carry

    for slot in range(per_dev):

        def send(r, carry):
            peer = lax.rem(me + r * (members // 2 - 1), members)
            pltpu.make_async_remote_copy(
                src_ref=packed.at[peer * per_dev + slot],
                dst_ref=heads_in.at[slot, my_position],
                send_sem=qkv_send.at[slot],
                recv_sem=qkv_recv.at[slot],
                device_id={"seq": peer},
                device_id_type=MESH,
            ).start()
            return carry

        lax.fori_loop(1, members, send, 0)
        if slot == 0:
            lax.fori_loop(0, cols, swap_weight, 0)

    def own_weight(column, carry):
        pltpu.make_async_copy(
            weight.at[:, weight_columns(column, half)],
            wboth.at[pl.ds(0, out_cols), pl.ds(pl.multiple_of(column * depth, depth), depth)],
            w_local,
        ).start()
        return carry

    lax.fori_loop(0, cols, own_weight, 0)

    nblock = lists.shape[0]
    place = lax.broadcasted_iota(jnp.int32, (tokens, width), 0)
    lane = lax.broadcasted_iota(jnp.int32, (tokens, width), 1)
    token = block_at(place // tile, lax.rem(place, tile) // rows) * rows + lax.rem(place, rows)
    spatial = token // BLOCK
    temporal = lax.rem(token, tokens // FRAMES) // (BLOCK // FRAMES)
    every = lists[...].astype(jnp.float32)
    head_lane = lax.broadcasted_iota(jnp.int32, every.shape, 2)
    entry = lax.broadcasted_iota(jnp.int32, every.shape[:2] + (width,), 1)
    listed_lane = lax.broadcasted_iota(jnp.int32, entry.shape, 2).astype(jnp.float32)
    for slot in range(per_dev):
        head = me * per_dev + slot
        block_of = jnp.where(classes[0, head] == 1, temporal, spatial)
        member = jnp.where(block_of == lane, 1.0, 0.0).astype(jnp.bfloat16)
        ebuf[slot] = member
        entries = jnp.sum(jnp.where(head_lane == head, every, 0.0), axis=2, keepdims=True)
        usable = jnp.where(entry < counts[0, head], 0.0, -MASKED)
        offset = jnp.max(jnp.where(entries == listed_lane, usable, -MASKED), axis=1)
        offset = jnp.concatenate(
            [offset, jnp.zeros((width - nblock, width), jnp.float32)], axis=0
        ).astype(jnp.bfloat16)
        bbuf[slot] = lax.dot_general(
            member, offset, (((1,), (1,)), ((), ())), preferred_element_type=jnp.float32
        ).astype(jnp.bfloat16)
    for copy in own_copies:
        copy.wait()

    scale = LOG2E * width ** (-0.5)
    others = pl.ds(0, members - 1)

    def chunk_rows(chunk):
        return pl.ds(pl.multiple_of(chunk * tile, tile), tile)

    def piece_copy(source_level, slot, chunk, target, sems):
        column = 2 * source_level + side
        piece = abuf.at[column, slot, chunk_rows(chunk)]
        return pltpu.make_async_remote_copy(
            src_ref=piece,
            dst_ref=piece,
            send_sem=sems.at[slot, chunk, source_level],
            recv_sem=a_recv.at[column, slot, chunk],
            device_id={"seq": target},
            device_id_type=MESH,
        )

    def received(column, slot, chunk):
        piece = abuf.at[column, slot, chunk_rows(chunk)]
        pltpu.make_async_copy(piece, piece, a_recv.at[column, slot, chunk]).wait()

    def send_up(source_level, slot, chunk):
        @pl.when(level + 1 < levels)
        def _():
            piece_copy(source_level, slot, chunk, me + 4, up_send).start()

    def send_down(source_level, slot, chunk):
        @pl.when(level >= 1)
        def _():
            piece_copy(source_level, slot, chunk, me - 4, down_send).start()

    def send_side(source_level, slot, chunk):
        piece_copy(source_level, slot, chunk, across, side_send).start()

    def attend(slot, then):
        span = heads_in.at[slot, others]
        pltpu.make_async_copy(span, span, qkv_recv.at[slot]).wait()

        def step(chunk, carry):
            here = chunk_rows(chunk)
            query = heads_in[slot, pl.ds(chunk * group, group), 0].reshape(tile, width)
            key = heads_in[slot, :, 1].reshape(tokens, width)
            value = heads_in[slot, :, 2].reshape(tokens, width)
            wide_query = jnp.concatenate([query, ebuf[slot, here]], axis=1)
            wide_key = jnp.concatenate([key, bbuf[slot]], axis=1)
            scores = lax.dot_general(
                wide_query, wide_key, (((1,), (1,)), ((), ())), preferred_element_type=jnp.float32
            )
            top = jnp.max(scores, axis=1, keepdims=True)
            probs = jnp.exp2((scores - top) * scale).astype(jnp.bfloat16)
            wide_value = jnp.concatenate(
                [value, jnp.ones((tokens, width), jnp.bfloat16)], axis=1
            )
            sums = jnp.dot(probs, wide_value, preferred_element_type=jnp.float32)
            abuf[col, slot, here] = (sums[:, :width] / sums[:, width:]).astype(jnp.bfloat16)
            send_up(level, slot, chunk)
            send_down(level, slot, chunk)
            send_side(level, slot, chunk)
            if then is not None:
                then(chunk)
            return carry

        lax.fori_loop(0, chunks, step, 0)

    def relay(slot, chunk, first, last):
        def hop(t, carry):
            below = level - 1 - t
            above = level + 1 + t

            @pl.when(below >= 0)
            def _():
                received(2 * below + side, slot, chunk)
                send_up(below, slot, chunk)
                send_side(below, slot, chunk)

            @pl.when(above < levels)
            def _():
                received(2 * above + side, slot, chunk)
                send_down(above, slot, chunk)
                send_side(above, slot, chunk)

            return carry

        lax.fori_loop(first, last, hop, 0)

    def relay_all(slot, first, last):
        def step(chunk, carry):
            relay(slot, chunk, first, last)
            return carry

        lax.fori_loop(0, chunks, step, 0)

    weight_span = wboth.at[pl.ds(out_cols, out_cols)]
    for slot in range(per_dev):
        before = None
        if slot > 0:
            before = functools.partial(relay, slot - 1, first=1, last=2)
        attend(slot, before)
        if slot > 0:
            relay_all(slot - 1, 2, levels - 1)
        if slot < per_dev - 1:
            relay_all(slot, 0, 1)

    def wave(n, carry):
        def hop(t, inner):
            @pl.when((n >= t) & (n - t < chunks))
            def _():
                relay(per_dev - 1, n - t, t, t + 1)

            return inner

        return lax.fori_loop(0, levels - 1, hop, carry)

    lax.fori_loop(0, levels - 1, wave, 0)
    weight_own = wboth.at[pl.ds(0, out_cols)]
    pltpu.make_async_copy(weight_own, weight_own, w_local).wait()
    pltpu.make_async_copy(weight_span, weight_span, w_sems.at[1]).wait()

    def chunk_copy(chunk):
        here = chunk_rows(chunk)
        return pltpu.make_async_remote_copy(
            src_ref=csend.at[here],
            dst_ref=crecv.at[here],
            send_sem=c_send.at[chunk],
            recv_sem=c_recv.at[chunk],
            device_id={"seq": partner},
            device_id_type=MESH,
        )

    def row_copy(chunk, q):
        start = pl.multiple_of((chunk * group + q) * rows, rows)
        return pltpu.make_async_remote_copy(
            src_ref=osend.at[pl.ds(start, rows)],
            dst_ref=obuf.at[me],
            send_sem=o_send.at[chunk * group + q],
            recv_sem=o_recv.at[me],
            device_id=(following, block_at(chunk, q)),
            device_id_type=MESH,
        )

    def hand(chunk):
        here = chunk_rows(chunk)
        chunk_copy(chunk).wait_recv()
        osend[here] = (cown[here] + crecv[here].astype(jnp.float32)).astype(jnp.bfloat16)
        for q in range(group):
            row_copy(chunk, lax.rem(level + q, group)).start()

    def finish(chunk, carry):
        here = chunk_rows(chunk)

        wave(chunk + levels - 1, 0)

        def from_side(source_level, inner):
            for slot in range(per_dev):
                received(2 * source_level + 1 - side, slot, chunk)
            return inner

        lax.fori_loop(0, levels, from_side, 0)
        piece = jnp.concatenate(
            [abuf[column, slot, here] for column in range(cols) for slot in range(per_dev)], axis=1
        )
        shares = lax.dot_general(
            piece, wboth[...], (((1,), (1,)), ((), ())), preferred_element_type=jnp.float32
        )
        csend[here] = shares[:, out_cols:].astype(jnp.bfloat16)
        chunk_copy(chunk).start()
        cown[here] = shares[:, :out_cols]

        @pl.when(chunk >= 1)
        def _():
            hand(chunk - 1)

        return carry

    lax.fori_loop(0, chunks, finish, 0)
    hand(chunks - 1)

    for slot in range(per_dev):
        span = heads_in.at[slot, others]
        pltpu.make_async_copy(span, span, qkv_send.at[slot]).wait()
    pltpu.make_async_copy(weight_span, weight_span, w_sems.at[0]).wait()

    def left(chunk, carry):
        for slot in range(per_dev):

            def from_level(source_level, inner):
                @pl.when((level + 1 < levels) & (source_level <= level))
                def _():
                    piece_copy(source_level, slot, chunk, across, up_send).wait_send()

                @pl.when((level >= 1) & (source_level >= level))
                def _():
                    piece_copy(source_level, slot, chunk, across, down_send).wait_send()

                piece_copy(source_level, slot, chunk, across, side_send).wait_send()
                return inner

            lax.fori_loop(0, levels, from_level, 0)
        chunk_copy(chunk).wait_send()
        for q in range(group):
            row_copy(chunk, q).wait_send()
        return carry

    lax.fori_loop(0, chunks, left, 0)

    def arrived(source, carry):
        pltpu.make_async_copy(obuf.at[source], obuf.at[source], o_recv.at[source]).wait()
        return carry

    lax.fori_loop(0, members, arrived, 0)
    pair = 2 * out_cols
    for i in range(members // 2):
        out[:, i * pair : (i + 1) * pair] = jnp.concatenate([obuf[2 * i], obuf[2 * i + 1]], axis=1)


def shards(stages, queries, keys, values, out_weight, head_class, kv_blocks, kv_count):
    members = lax.axis_size("seq")
    heads = head_class.shape[1]
    per_dev = heads // members
    rows, total = queries.shape[1:]
    width = total // heads
    tokens = rows * members
    out_cols = out_weight.shape[2]
    cols = members // 2
    depth = per_dev * width
    weight = out_weight[0].T
    bf16, f32 = jnp.bfloat16, jnp.float32
    dma = pltpu.SemaphoreType.DMA
    vmem = pl.BlockSpec(memory_space=pltpu.VMEM)
    smem = pl.BlockSpec(memory_space=pltpu.SMEM)
    hbm = pl.BlockSpec(memory_space=pl.ANY)
    head_buffer = pltpu.VMEM((per_dev, tokens, width), bf16)
    levels = members // 4
    chunks = tokens // TILE
    result = pl.pallas_call(
        functools.partial(kernel, members, per_dev, stages),
        out_shape=jax.ShapeDtypeStruct((rows, members * out_cols), bf16),
        in_specs=[smem, smem, vmem, hbm, hbm, hbm, hbm],
        out_specs=vmem,
        scratch_shapes=[
            pltpu.VMEM((3, rows, total), bf16),
            pltpu.VMEM((heads, 3, rows, width), bf16),
            pltpu.VMEM((per_dev, members, 3, rows, width), bf16),
            head_buffer, head_buffer,
            pltpu.VMEM((cols, per_dev, tokens, width), bf16),
            pltpu.VMEM((2 * out_cols, cols * depth), bf16),
            pltpu.VMEM((tokens, out_cols), f32),
            pltpu.VMEM((tokens, out_cols), bf16),
            pltpu.VMEM((tokens, out_cols), bf16),
            pltpu.VMEM((tokens, out_cols), bf16),
            pltpu.VMEM((members, rows, out_cols), bf16),
            dma((3,)), dma((per_dev,)), dma((per_dev,)), dma((per_dev,)),
            dma((2,)), dma,
            dma((per_dev, chunks, levels)), dma((per_dev, chunks, levels)),
            dma((per_dev, chunks, levels)), dma((cols, per_dev, chunks)),
            dma((chunks,)), dma((chunks,)),
            dma((members,)), dma((members,)),
        ],
        compiler_params=pltpu.CompilerParams(
            collective_id=0, has_side_effects=True, vmem_limit_bytes=60 * 1024 * 1024
        ),
        cost_estimate=pl.CostEstimate(
            flops=4 * tokens * tokens * depth + 2 * tokens * total * out_cols,
            bytes_accessed=2 * (3 * rows * total + total * out_cols + rows * members * out_cols),
            transcendentals=per_dev * tokens * tokens,
        ),
    )(head_class, kv_count, kv_blocks[0].transpose(1, 2, 0), queries[0], keys[0], values[0], weight)
    return result[None]


def solution(mesh):
    placed = (
        P("pipe", "seq", None),
        P("pipe", "seq", None),
        P("pipe", "seq", None),
        P("pipe", None, "seq"),
        P("pipe", None),
        P("pipe", None, None, None),
        P("pipe", None),
    )
    return jax.shard_map(
        functools.partial(shards, mesh.shape["pipe"]),
        mesh=mesh, in_specs=placed, out_specs=P("pipe", "seq", None), check_vma=False,
    )
```
